256 devices in a mesh: grp: 16 (over y_hi, z), dev: 16 (over y_lo, x, core).
Axes of the slice: x: 4, y: 4 (y_hi: 2, y_lo: 2; y = y_hi * 2 + y_lo), z: 8, core: 2. Of those that a mesh axis runs over, the one named last changes fastest.
Arguments:
- spatial_basis: bfloat16 [2, 32, 2, 192, 192], P(None, None, None, 'dev'), may hold values from -6 to 6
- temporal: bfloat16 [2, 32, 256], replicated, may hold values from -1 to 1
- coil_maps: bfloat16 [2, 16, 2, 192, 192], replicated, may hold values from -1.5 to 1.5
- kspace_data: float32 [256, 2, 16, 2, 48, 192], P(('grp', 'dev')), may hold values from -6 to 6
- sampled_lines: int32 [256, 48], P(('grp', 'dev')), may hold values from 0 to 191, as said below
Outputs:
- updated_basis: float32 [2, 32, 2, 192, 192], P(None, None, None, 'dev', 'grp')
The draws below stay inside these ranges and needn't reach their ends.
Inputs may be any that keep to these rules, and one draw needn't show every extreme that they name: `sampled_lines`: each row holds 48 different line indices of one frame.
All inputs are finite; a program needn't handle non-finite values.
Results may differ from the reference program's by a relative error of at most 0.0004.
Values may be sent and summed in bfloat16 or wider, within the bound.
No kernel may reach another device: no remote copies, remote signals or barrier semaphores. Data moves between devices by JAX's collectives and lax.ppermute only.
A program may use at most 128 MiB of HBM per device.

```python
import jax
import jax.numpy as jnp
from jax import lax

NY = 192
NZ = 192
L = 32
C = 16
XW = 2
LINES = 48
FRAMES = 256


def draw_sampled_lines(key, part):
    key = jax.random.fold_in(key, 11)
    frame_keys = jax.random.split(key, FRAMES)

    def one_frame(frame_key):
        return jax.random.permutation(frame_key, NY)[:LINES]
    return jax.vmap(one_frame)(frame_keys).astype(jnp.int32)


def block_scale(rng, shape, pieces, smallest, largest):
    loudness, own = 1.0, jax.random.fold_in(rng, 6)
    for dim, shards_of in pieces:
        heights = jnp.exp(jax.random.uniform(jax.random.fold_in(own, dim), (shards_of,), jnp.float32, smallest / len(pieces), largest / len(pieces)))
        loudness = loudness * jnp.repeat(heights, shape[dim] // shards_of).reshape([-1 if axis == dim else 1 for axis in range(len(shape))])
    return loudness


def bell_draw(own_key, dims, spread, most, pieces=(), held_as=jnp.bfloat16):
    factor_of = block_scale(own_key, dims, pieces, -0.22, 0.18) if pieces else 1.0
    values = jax.random.normal(own_key, dims, jnp.float32) * spread * factor_of
    return jnp.minimum(jnp.maximum(values, -most), most).astype(held_as)


def setup_inputs(seed: int = 0) -> dict:
    seeds = jax.random.split(jax.random.key(seed), 6)
    return {
        "spatial_basis": bell_draw(seeds[0], (2, L, XW, NY, NZ), 1.0, 6.0, ((3, 16),)),
        "temporal": bell_draw(seeds[1], (2, L, FRAMES), L ** -0.5, 1.0),
        "coil_maps": bell_draw(seeds[2], (2, C, XW, NY, NZ), 0.25, 1.5),
        "kspace_data": bell_draw(seeds[3], (FRAMES, 2, C, XW, LINES, NZ), 1.0, 6.0, ((0, 256),), jnp.float32),
        "sampled_lines": draw_sampled_lines(jax.random.fold_in(seeds[5], 71), 0),
    }


PRECISE = lax.Precision.HIGHEST
STEP_SIZE = 0.25


def reference(spatial_basis, temporal, coil_maps, kspace_data, sampled_lines):
    basis_re = spatial_basis[0].astype(jnp.float32)
    basis_im = spatial_basis[1].astype(jnp.float32)
    coil_field = lax.complex(coil_maps[0].astype(jnp.float32), coil_maps[1].astype(jnp.float32))
    temp_re = jnp.transpose(temporal[0].astype(jnp.float32))
    temp_im = jnp.transpose(temporal[1].astype(jnp.float32))

    def one_frame(gradient, inputs):
        weight_re, weight_im, frame_data, line_ids = inputs
        image_re = jnp.einsum("lxyz,l->xyz", basis_re, weight_re, precision=PRECISE) - jnp.einsum("lxyz,l->xyz", basis_im, weight_im, precision=PRECISE)
        image_im = jnp.einsum("lxyz,l->xyz", basis_re, weight_im, precision=PRECISE) + jnp.einsum("lxyz,l->xyz", basis_im, weight_re, precision=PRECISE)
        coil_images = coil_field * lax.complex(image_re, image_im)[None]
        rows_full = jnp.fft.fft(coil_images, axis=2, norm="ortho")
        sampled = jnp.take(rows_full, line_ids, axis=2)
        kspace = jnp.fft.fft(sampled, axis=3, norm="ortho")
        residual = kspace - lax.complex(frame_data[0], frame_data[1])
        back_depth = jnp.fft.ifft(residual, axis=3, norm="ortho")
        filled = jnp.zeros_like(coil_images).at[:, :, line_ids, :].add(back_depth)
        back_rows = jnp.fft.ifft(filled, axis=2, norm="ortho")
        frame_grad = jnp.sum(jnp.conj(coil_field) * back_rows, axis=0)
        weight = lax.complex(weight_re, weight_im)
        gradient = gradient + frame_grad[None] * jnp.conj(weight)[:, None, None, None]
        return gradient, None

    zero_field = jnp.zeros((L, XW, NY, NZ), jnp.float32)
    initial = lax.complex(zero_field, zero_field)
    gradient, unused = lax.scan(one_frame, initial, (temp_re, temp_im, kspace_data, sampled_lines))
    update_re = basis_re - STEP_SIZE * jnp.real(gradient)
    update_im = basis_im - STEP_SIZE * jnp.imag(gradient)
    return jnp.stack([update_re, update_im])
```

```python
import math

import jax
import jax.numpy as jnp
import numpy as np
from jax import lax
from jax.experimental import pallas as pl
from jax.experimental.pallas import tpu as pltpu
from jax.sharding import PartitionSpec as P

STEP_SIZE = 0.25
N = 192
PART = 12
RANK = 32
COILS = 16
LINES = 48
GROUP = 16
VOX = 2 * 2 * PART * PART
WIDE = 640
F32 = jnp.float32
BF16 = jnp.bfloat16
VMEM = pl.BlockSpec(memory_space=pltpu.VMEM)


def two_terms(values):
    high = values.astype(np.float32).astype(jnp.bfloat16)
    low = (values - high.astype(np.float64)).astype(jnp.bfloat16)
    return high, low


def split(values):
    high = values.astype(BF16)
    return high, (values - high.astype(F32)).astype(BF16)


def dot(left, right, over=(1, 0)):
    return lax.dot_general(
        left, right, (((over[0],), (over[1],)), ((), ())), preferred_element_type=F32
    )


def constants():
    places = np.arange(N)
    angles = (places[:, None] * places[None, :] % N) * (2.0 * math.pi / N)
    cos_pair = two_terms(np.cos(angles) / math.sqrt(N))
    sin_pair = two_terms(np.sin(angles) / math.sqrt(N))
    dft = np.stack([*cos_pair, *sin_pair])
    columns = np.arange(2 * RANK * 2 * PART)
    spread = (columns[None, :] // (2 * PART) == np.arange(2 * RANK)[:, None])
    rows = np.arange(2 * PART)
    inside = (columns[None, :] % (2 * PART) == ((rows % PART) * 2 + rows // PART)[:, None])
    order = np.arange(N)
    depth_order = ((order % GROUP) * PART + order // GROUP)[:, None] == places[None, :]
    wide = np.arange(4 * N)
    target = (wide // PART % GROUP) * (4 * PART) + (wide // N) * PART + wide % PART
    lane_order = target[:, None] == wide[None, :]
    peers = np.arange(GROUP * GROUP)
    frame_order = ((peers % GROUP) * GROUP + peers // GROUP)[:, None] == peers[None, :]
    out = np.arange(2 * PART * PART)
    row, zz, pos = out // (2 * PART), out // 2 % PART, out % 2
    pick = np.stack(
        [
            (zz * 48 + part * 24 + pos * PART + row)[:, None] == np.arange(WIDE)[None, :]
            for part in range(2)
        ]
    )
    return dict(
        dft=dft,
        spread=spread.astype(jnp.bfloat16),
        inside=inside.astype(np.float32),
        depth_order=depth_order.astype(jnp.bfloat16),
        lane_order=lane_order.astype(jnp.bfloat16),
        frame_order=frame_order.astype(jnp.bfloat16),
        pick=pick.astype(jnp.bfloat16),
    )


def frames_kernel(basis_ref, temporal_ref, spread_ref, inside_ref, out_ref, mix_ref):
    first = lax.axis_index("grp") * GROUP
    frame = lax.broadcasted_iota(jnp.int32, (GROUP, GROUP * GROUP), 0) + first
    column = lax.broadcasted_iota(jnp.int32, (GROUP, GROUP * GROUP), 1)
    chosen = (frame == column).astype(F32).astype(BF16)
    weights = dot(chosen, temporal_ref[...], (1, 1))
    lane = lax.broadcasted_iota(jnp.int32, (GROUP, 2 * RANK), 1)
    from_lane = lax.broadcasted_iota(jnp.int32, (2 * RANK, 2 * RANK), 0)
    to_lane = lax.broadcasted_iota(jnp.int32, (2 * RANK, 2 * RANK), 1)
    apart = jnp.abs(from_lane - to_lane) == RANK
    swapped = dot(weights.astype(BF16), apart.astype(F32).astype(BF16))
    signed = jnp.where(lane < RANK, weights, -weights)
    wide_re = dot(signed.astype(BF16), spread_ref[...])
    wide_im = dot(swapped.astype(BF16), spread_ref[...])
    inside = inside_ref[...]
    for f in range(GROUP):
        block = jnp.concatenate(
            [inside * wide_re[f : f + 1], inside * wide_im[f : f + 1]], axis=0
        )
        mix_ref[f * 48 : (f + 1) * 48, :] = block.astype(BF16)
    images = dot(mix_ref[...], basis_ref[...])
    for f in range(GROUP):
        image = images[f * 48 : (f + 1) * 48]
        out_ref[f, 0:48, :] = image[:, 0:128]
        out_ref[f, 48:72, 0:64] = image[0:24, 128:192]
        out_ref[f, 48:72, 64:128] = image[24:48, 128:192]


def frames(basis, temporal, spread, inside):
    rows = 2 * RANK * 2 * PART
    return pl.pallas_call(
        frames_kernel,
        out_shape=jax.ShapeDtypeStruct((GROUP, 72, 128), F32),
        in_specs=[VMEM] * 4,
        out_specs=VMEM,
        scratch_shapes=[pltpu.VMEM((GROUP * 48, rows), BF16)],
        compiler_params=pltpu.CompilerParams(vmem_limit_bytes=24 * 1024 * 1024),
        name="frames",
    )(basis, temporal, spread, inside)


def data_kernel(
    data_ref, lines_ref, dft_ref, temporal_ref, order_ref,
    back_ref, ahead_ref, adjoint_ref, low_ref, weights_ref,
):
    step = pl.program_id(0)

    @pl.when(step == 0)
    def tables():
        places = lax.broadcasted_iota(jnp.int32, (N, LINES), 0)
        chosen = (places == lines_ref[...]).astype(F32)
        chosen_rows = chosen.T.astype(BF16)
        chosen = chosen.astype(BF16)
        for term in range(2):
            cos_line = dot(chosen_rows, dft_ref[term])
            sin_line = dot(chosen_rows, dft_ref[2 + term])
            at = term * 96
            ahead_ref[at : at + 96, 0:N] = jnp.concatenate([cos_line, -sin_line], 0).astype(BF16)
            ahead_ref[at : at + 96, N : 2 * N] = jnp.concatenate([sin_line, cos_line], 0).astype(BF16)
            cos_back = dot(dft_ref[term], chosen)
            sin_back = dot(dft_ref[2 + term], chosen)
            full = jnp.concatenate(
                [
                    jnp.concatenate([cos_back, -sin_back], 1),
                    jnp.concatenate([sin_back, cos_back], 1),
                ],
                0,
            ).astype(BF16)
            if term == 0:
                adjoint_ref[:, 0:96] = full
                adjoint_ref[:, 96:192] = full
            else:
                low_ref[...] = full
        weights_ref[...] = dot(order_ref[...], temporal_ref[...], (1, 1)).astype(BF16)

    coils_here = data_ref.shape[2]
    data_re = data_ref[0, 0].reshape(coils_here * 2 * LINES, N)
    data_im = data_ref[0, 1].reshape(coils_here * 2 * LINES, N)
    re_high, re_low = split(data_re)
    im_high, im_low = split(data_im)

    def through(high, low, which):
        return (
            dot(high, dft_ref[which])
            + dot(low, dft_ref[which])
            + dot(high, dft_ref[which + 1])
        )

    back_re = through(re_high, re_low, 0) - through(im_high, im_low, 2)
    back_im = through(re_high, re_low, 2) + through(im_high, im_low, 0)
    back_ref[:, 0:LINES, :] = back_re.reshape(coils_here * 2, LINES, N)
    back_ref[:, LINES : 2 * LINES, :] = back_im.reshape(coils_here * 2, LINES, N)


def data_back(data, lines, dft, temporal, order):
    coils_here = 4
    whole = lambda *shape: pl.BlockSpec(shape, lambda i: (0,) * len(shape))
    return pl.pallas_call(
        data_kernel,
        grid=(COILS // coils_here,),
        out_shape=(
            jax.ShapeDtypeStruct((COILS * 2, 2 * LINES, N), F32),
            jax.ShapeDtypeStruct((4 * LINES, 2 * N), BF16),
            jax.ShapeDtypeStruct((2 * N, 4 * LINES), BF16),
            jax.ShapeDtypeStruct((2 * N, 2 * LINES), BF16),
            jax.ShapeDtypeStruct((GROUP * GROUP, 2 * RANK), BF16),
        ),
        in_specs=[
            pl.BlockSpec((1, 2, coils_here, 2, LINES, N), lambda i: (0, 0, i, 0, 0, 0)),
            whole(1, LINES),
            whole(4, N, N),
            whole(2 * RANK, GROUP * GROUP),
            whole(GROUP * GROUP, GROUP * GROUP),
        ],
        out_specs=(
            pl.BlockSpec((coils_here * 2, 2 * LINES, N), lambda i: (i, 0, 0)),
            whole(4 * LINES, 2 * N),
            whole(2 * N, 4 * LINES),
            whole(2 * N, 2 * LINES),
            whole(GROUP * GROUP, 2 * RANK),
        ),
        compiler_params=pltpu.CompilerParams(vmem_limit_bytes=24 * 1024 * 1024),
        name="data_back",
    )(data, lines, dft, temporal, order)


def model_kernel(
    images_ref, coils_ref, back_ref, ahead_ref, adjoint_ref, low_ref,
    depth_ref, lane_ref, out_ref, field_ref, grad_ref,
):
    for d in range(GROUP):
        at = d * PART
        for part in range(2):
            for pos in range(2):
                row = part * 24 + pos * PART
                field_ref[part, pos, at : at + PART, 0:128] = images_ref[d, row : row + PART, :]
                tail = 48 + pos * PART
                field_ref[part, pos, at : at + PART, 128:N] = images_ref[
                    d, tail : tail + PART, part * 64 : part * 64 + 64
                ]
    grad_ref[...] = jnp.zeros_like(grad_ref)
    for pos in range(2):

        def one_coil(coil, carry):
            coil_re = coils_ref[0, coil, pos].astype(F32)
            coil_im = coils_ref[1, coil, pos].astype(F32)
            field_re = field_ref[0, pos]
            field_im = field_ref[1, pos]
            re_high, re_low = split(coil_re * field_re - coil_im * field_im)
            im_high, im_low = split(coil_re * field_im + coil_im * field_re)
            high = jnp.concatenate([re_high, im_high], 0)
            low = jnp.concatenate([re_low, im_low], 0)
            first = dot(ahead_ref[...], high)
            lines = first[0:96] + first[96:192] + dot(ahead_ref[0:96, :], low)
            resid_high, resid_low = split(lines - back_ref[coil * 2 + pos])
            rows = dot(adjoint_ref[...], jnp.concatenate([resid_high, resid_low], 0))
            rows = rows + dot(low_ref[...], resid_high)
            rows_re, rows_im = rows[0:N], rows[N : 2 * N]
            grad_ref[0, pos] += coil_re * rows_re + coil_im * rows_im
            grad_ref[1, pos] += coil_re * rows_im - coil_im * rows_re
            return carry

        lax.fori_loop(0, COILS, one_coil, 0)
    highs, lows = [], []
    for part in range(2):
        for pos in range(2):
            high, low = split(grad_ref[part, pos])
            highs.append(dot(depth_ref[...], high, (1, 1)).astype(BF16))
            lows.append(dot(depth_ref[...], low, (1, 1)).astype(BF16))
    total = jnp.zeros((N, 4 * N), F32)
    for channel in range(4):
        order = lane_ref[channel * N : (channel + 1) * N, :]
        total = total + dot(highs[channel], order) + dot(lows[channel], order)
    for d in range(GROUP):
        out_ref[d * GROUP : (d + 1) * GROUP, 0:VOX] = jnp.concatenate(
            [total[zz * GROUP : (zz + 1) * GROUP, d * 48 : (d + 1) * 48] for zz in range(PART)], 1
        )
    out_ref[:, VOX:WIDE] = jnp.zeros((GROUP * GROUP, WIDE - VOX), F32)


def model(images, coils, back, ahead, adjoint, low, depth_order, lane_order):
    return pl.pallas_call(
        model_kernel,
        out_shape=jax.ShapeDtypeStruct((GROUP * GROUP, WIDE), F32),
        in_specs=[VMEM] * 8,
        out_specs=VMEM,
        scratch_shapes=[
            pltpu.VMEM((2, 2, N, N), F32),
            pltpu.VMEM((2, 2, N, N), F32),
        ],
        compiler_params=pltpu.CompilerParams(vmem_limit_bytes=40 * 1024 * 1024),
        name="model",
    )(images, coils, back, ahead, adjoint, low, depth_order, lane_order)


def update_kernel(grads_ref, weights_ref, pick_ref, slab_ref, out_ref):
    high, low = split(grads_ref[...].T)
    weights = weights_ref[...]
    both = dot(high, weights) + dot(low, weights)
    high, low = split(both)
    from_re = dot(pick_ref[0], high) + dot(pick_ref[0], low)
    from_im = dot(pick_ref[1], high) + dot(pick_ref[1], low)
    grad_re = from_re[:, 0:RANK] + from_im[:, RANK : 2 * RANK]
    grad_im = from_im[:, 0:RANK] - from_re[:, RANK : 2 * RANK]
    out_ref[0] = slab_ref[0] - STEP_SIZE * grad_re
    out_ref[1] = slab_ref[1] - STEP_SIZE * grad_im


def update(grads, weights, pick, slab):
    return pl.pallas_call(
        update_kernel,
        out_shape=jax.ShapeDtypeStruct((2, 2 * PART * PART, RANK), F32),
        in_specs=[VMEM] * 4,
        out_specs=VMEM,
        compiler_params=pltpu.CompilerParams(vmem_limit_bytes=16 * 1024 * 1024),
        name="update",
    )(grads, weights, pick, slab)


def on_device(spatial_basis, temporal, coil_maps, kspace_data, sampled_lines):
    table = {name: jnp.asarray(value) for name, value in constants().items()}
    flat_temporal = temporal.reshape(2 * RANK, GROUP * GROUP)
    flat_basis = jnp.transpose(spatial_basis, (0, 1, 3, 2, 4)).reshape(-1, N)
    sent = frames(flat_basis, flat_temporal, table["spread"], table["inside"])
    images = lax.all_to_all(sent, "dev", 0, 0, tiled=True)
    back, ahead, adjoint, low, weights = data_back(
        kspace_data, sampled_lines, table["dft"], flat_temporal, table["frame_order"]
    )
    sent = model(
        images, coil_maps, back, ahead, adjoint, low, table["depth_order"], table["lane_order"]
    )
    grads = lax.all_to_all(
        sent.reshape(GROUP * GROUP, 1, WIDE), ("dev", "grp"), 0, 0, tiled=True
    )
    slab = lax.dynamic_slice_in_dim(spatial_basis, lax.axis_index("grp") * PART, PART, 4)
    slab = jnp.transpose(slab, (0, 3, 4, 2, 1)).reshape(2, 2 * PART * PART, RANK).astype(F32)
    result = update(grads.reshape(GROUP * GROUP, WIDE), weights, table["pick"], slab)
    return jnp.transpose(result.reshape(2, PART, PART, 2, RANK), (0, 4, 3, 1, 2))


def solution(mesh):
    placed = (
        P(None, None, None, "dev", None),
        P(),
        P(),
        P(("grp", "dev"), None, None, None, None, None),
        P(("grp", "dev"), None),
    )
    return jax.shard_map(
        on_device,
        mesh=mesh,
        in_specs=placed,
        out_specs=P(None, None, None, "dev", "grp"),
        check_vma=False,
    )
```

```python
import math

import jax
import jax.numpy as jnp
import numpy as np
from jax import lax
from jax.experimental import pallas as pl
from jax.experimental.pallas import tpu as pltpu
from jax.sharding import PartitionSpec as P

STEP_SIZE = 0.25
N = 192
PART = 12
RANK = 32
COILS = 16
LINES = 48
CHUNK = 4
GROUP = 16
VOX = 2 * 2 * PART * PART
WIDE = 640
F32 = jnp.float32
BF16 = jnp.bfloat16
VMEM = pl.BlockSpec(memory_space=pltpu.VMEM)
HBM = pl.BlockSpec(memory_space=pltpu.HBM)
in_hbm = lambda array: pltpu.with_memory_space_constraint(array, pltpu.HBM)
in_vmem = lambda array: pltpu.with_memory_space_constraint(array, pltpu.VMEM)
DMA = pltpu.SemaphoreType.DMA
MIB = 1024 * 1024


def two_terms(values):
    high = values.astype(np.float32).astype(jnp.bfloat16)
    low = (values - high.astype(np.float64)).astype(jnp.bfloat16)
    return high, low


def split(values):
    high = values.astype(BF16)
    return high, (values - high.astype(F32)).astype(BF16)


def dot(left, right, over=(1, 0)):
    return lax.dot_general(
        left, right, (((over[0],), (over[1],)), ((), ())), preferred_element_type=F32
    )


def constants():
    places = np.arange(N)
    angles = (places[:, None] * places[None, :] % N) * (2.0 * math.pi / N)
    cos_pair = two_terms(np.cos(angles) / math.sqrt(N))
    sin_pair = two_terms(np.sin(angles) / math.sqrt(N))
    dft = np.stack([*cos_pair, *sin_pair])
    columns = np.arange(2 * RANK * 2 * PART)
    spread = (columns[None, :] // (2 * PART) == np.arange(2 * RANK)[:, None])
    rows = np.arange(2 * PART)
    inside = (columns[None, :] % (2 * PART) == ((rows % PART) * 2 + rows // PART)[:, None])
    order = np.arange(N)
    depth_order = ((order % GROUP) * PART + order // GROUP)[:, None] == places[None, :]
    wide = np.arange(4 * N)
    target = (wide // PART % GROUP) * (4 * PART) + (wide // N) * PART + wide % PART
    lane_order = target[:, None] == wide[None, :]
    peers = np.arange(GROUP * GROUP)
    frame_order = ((peers % GROUP) * GROUP + peers // GROUP)[:, None] == peers[None, :]
    out = np.arange(2 * PART * PART)
    row, zz, pos = out // (2 * PART), out // 2 % PART, out % 2
    pick = np.stack(
        [
            (zz * 48 + part * 24 + pos * PART + row)[:, None] == np.arange(WIDE)[None, :]
            for part in range(2)
        ]
    )
    return dict(
        dft=dft,
        spread=spread.astype(jnp.bfloat16),
        inside=inside.astype(np.float32),
        depth_order=depth_order.astype(jnp.bfloat16),
        lane_order=lane_order.astype(jnp.bfloat16),
        frame_order=frame_order.astype(jnp.bfloat16),
        pick=pick.astype(jnp.bfloat16),
    )


def frames_kernel(
    basis_ref, temporal_hbm, spread_hbm, inside_hbm, out_ref,
    temporal_ref, spread_ref, inside_ref, mix_ref, sems,
):
    copies = [
        pltpu.make_async_copy(source, target, sems.at[i])
        for i, (source, target) in enumerate(
            [(temporal_hbm, temporal_ref), (spread_hbm, spread_ref), (inside_hbm, inside_ref)]
        )
    ]
    for copy in copies:
        copy.start()
    copies[0].wait()
    first = lax.axis_index("grp") * GROUP
    frame = lax.broadcasted_iota(jnp.int32, (GROUP, GROUP * GROUP), 0) + first
    column = lax.broadcasted_iota(jnp.int32, (GROUP, GROUP * GROUP), 1)
    chosen = (frame == column).astype(F32).astype(BF16)
    weights = dot(chosen, temporal_ref[...], (1, 1))
    lane = lax.broadcasted_iota(jnp.int32, (GROUP, 2 * RANK), 1)
    from_lane = lax.broadcasted_iota(jnp.int32, (2 * RANK, 2 * RANK), 0)
    to_lane = lax.broadcasted_iota(jnp.int32, (2 * RANK, 2 * RANK), 1)
    apart = jnp.abs(from_lane - to_lane) == RANK
    swapped = dot(weights.astype(BF16), apart.astype(F32).astype(BF16))
    copies[1].wait()
    signed = jnp.where(lane < RANK, weights, -weights)
    wide_re = dot(signed.astype(BF16), spread_ref[...])
    wide_im = dot(swapped.astype(BF16), spread_ref[...])
    copies[2].wait()
    inside = inside_ref[...]
    for f in range(GROUP):
        block = jnp.concatenate(
            [inside * wide_re[f : f + 1], inside * wide_im[f : f + 1]], axis=0
        )
        mix_ref[f * 48 : (f + 1) * 48, :] = block.astype(BF16)
    images = dot(mix_ref[...], basis_ref[...])
    for f in range(GROUP):
        image = images[f * 48 : (f + 1) * 48]
        out_ref[f, 0:48, :] = image[:, 0:128]
        out_ref[f, 48:72, 0:64] = image[0:24, 128:192]
        out_ref[f, 48:72, 64:128] = image[24:48, 128:192]


def frames(basis, temporal, spread, inside):
    rows = 2 * RANK * 2 * PART
    return pl.pallas_call(
        frames_kernel,
        out_shape=jax.ShapeDtypeStruct((GROUP, 72, 128), F32),
        in_specs=[VMEM, HBM, HBM, HBM],
        out_specs=VMEM,
        scratch_shapes=[
            pltpu.VMEM((2 * RANK, GROUP * GROUP), BF16),
            pltpu.VMEM((2 * RANK, rows), BF16),
            pltpu.VMEM((2 * PART, rows), F32),
            pltpu.VMEM((GROUP * 48, rows), BF16),
            DMA((3,)),
        ],
        compiler_params=pltpu.CompilerParams(vmem_limit_bytes=12 * MIB),
        name="frames",
    )(basis, *map(in_hbm, (temporal, spread, inside)))


def data_kernel(
    data_hbm, lines_hbm, dft_hbm, temporal_hbm, order_hbm,
    back_ref, ahead_ref, adjoint_ref, low_ref, weights_ref,
    data_ref, lines_ref, dft_ref, temporal_ref, order_ref, data_sems, sems,
):
    small = [
        pltpu.make_async_copy(source, target, sems.at[i])
        for i, (source, target) in enumerate(
            [
                (dft_hbm, dft_ref),
                (lines_hbm, lines_ref),
                (temporal_hbm, temporal_ref),
                (order_hbm, order_ref),
            ]
        )
    ]
    chunks = [
        pltpu.make_async_copy(
            data_hbm.at[0, :, pl.ds(i * CHUNK, CHUNK)],
            data_ref.at[:, pl.ds(i * CHUNK, CHUNK)],
            data_sems.at[i],
        )
        for i in range(COILS // CHUNK)
    ]
    small[0].start()
    small[1].start()
    chunks[0].start()
    for copy in small[2:] + chunks[1:]:
        copy.start()
    small[0].wait()
    small[1].wait()
    places = lax.broadcasted_iota(jnp.int32, (N, LINES), 0)
    chosen = (places == lines_ref[...]).astype(F32)
    chosen_rows = chosen.T.astype(BF16)
    chosen = chosen.astype(BF16)
    for term in range(2):
        cos_line = dot(chosen_rows, dft_ref[term])
        sin_line = dot(chosen_rows, dft_ref[2 + term])
        at = term * 96
        ahead_ref[at : at + 96, 0:N] = jnp.concatenate([cos_line, -sin_line], 0).astype(BF16)
        ahead_ref[at : at + 96, N : 2 * N] = jnp.concatenate([sin_line, cos_line], 0).astype(BF16)
        cos_back = dot(dft_ref[term], chosen)
        sin_back = dot(dft_ref[2 + term], chosen)
        full = jnp.concatenate(
            [
                jnp.concatenate([cos_back, -sin_back], 1),
                jnp.concatenate([sin_back, cos_back], 1),
            ],
            0,
        ).astype(BF16)
        if term == 0:
            adjoint_ref[:, 0:96] = full
            adjoint_ref[:, 96:192] = full
        else:
            low_ref[...] = full

    def through(high, low, which):
        return (
            dot(high, dft_ref[which])
            + dot(low, dft_ref[which])
            + dot(high, dft_ref[which + 1])
        )

    for i in range(COILS // CHUNK):
        chunks[i].wait()
        here = slice(i * CHUNK, (i + 1) * CHUNK)
        re_high, re_low = split(data_ref[0, here].reshape(CHUNK * 2 * LINES, N))
        im_high, im_low = split(data_ref[1, here].reshape(CHUNK * 2 * LINES, N))
        back_re = through(re_high, re_low, 0) - through(im_high, im_low, 2)
        back_im = through(re_high, re_low, 2) + through(im_high, im_low, 0)
        pairs = slice(i * CHUNK * 2, (i + 1) * CHUNK * 2)
        back_ref[pairs, 0:LINES, :] = back_re.reshape(CHUNK * 2, LINES, N)
        back_ref[pairs, LINES : 2 * LINES, :] = back_im.reshape(CHUNK * 2, LINES, N)
    small[2].wait()
    small[3].wait()
    weights_ref[...] = dot(order_ref[...], temporal_ref[...], (1, 1)).astype(BF16)


def data_back(data, lines, dft, temporal, order):
    return pl.pallas_call(
        data_kernel,
        out_shape=(
            pltpu.VMEM((COILS * 2, 2 * LINES, N), F32),
            pltpu.VMEM((4 * LINES, 2 * N), BF16),
            pltpu.VMEM((2 * N, 4 * LINES), BF16),
            pltpu.VMEM((2 * N, 2 * LINES), BF16),
            pltpu.VMEM((GROUP * GROUP, 2 * RANK), BF16),
        ),
        in_specs=[HBM] * 5,
        out_specs=(VMEM,) * 5,
        scratch_shapes=[
            pltpu.VMEM((2, COILS, 2, LINES, N), F32),
            pltpu.VMEM((1, LINES), jnp.int32),
            pltpu.VMEM((4, N, N), BF16),
            pltpu.VMEM((2 * RANK, GROUP * GROUP), BF16),
            pltpu.VMEM((GROUP * GROUP, GROUP * GROUP), BF16),
            DMA((COILS // CHUNK,)),
            DMA((4,)),
        ],
        compiler_params=pltpu.CompilerParams(vmem_limit_bytes=16 * MIB),
        name="data_back",
    )(*map(in_hbm, (data, lines, dft, temporal, order)))


def model_kernel(
    images_ref, coils_hbm, back_ref, ahead_ref, adjoint_ref, low_ref, depth_hbm, lane_hbm,
    out_ref, coils_ref, depth_ref, lane_ref, field_ref, grad_ref, coil_sems, sems,
):
    half = COILS // 2

    def coil_copy(pos, side):
        here = pl.ds(side * half, half)
        return pltpu.make_async_copy(
            coils_hbm.at[:, here, pos], coils_ref.at[pos, :, here], coil_sems.at[pos, side]
        )

    orders = [
        pltpu.make_async_copy(depth_hbm, depth_ref, sems.at[0]),
        pltpu.make_async_copy(lane_hbm, lane_ref, sems.at[1]),
    ]
    for pos in range(2):
        for side in range(2):
            coil_copy(pos, side).start()
    for copy in orders:
        copy.start()
    for d in range(GROUP):
        at = d * PART
        for part in range(2):
            for pos in range(2):
                row = part * 24 + pos * PART
                field_ref[part, pos, at : at + PART, 0:128] = images_ref[d, row : row + PART, :]
                tail = 48 + pos * PART
                field_ref[part, pos, at : at + PART, 128:N] = images_ref[
                    d, tail : tail + PART, part * 64 : part * 64 + 64
                ]
    grad_ref[...] = jnp.zeros_like(grad_ref)
    for pos in range(2):

        def one_coil(coil, carry):
            coil_re = coils_ref[pos, 0, coil].astype(F32)
            coil_im = coils_ref[pos, 1, coil].astype(F32)
            field_re = field_ref[0, pos]
            field_im = field_ref[1, pos]
            re_high, re_low = split(coil_re * field_re - coil_im * field_im)
            im_high, im_low = split(coil_re * field_im + coil_im * field_re)
            high = jnp.concatenate([re_high, im_high], 0)
            low = jnp.concatenate([re_low, im_low], 0)
            first = dot(ahead_ref[...], high)
            lines = first[0:96] + first[96:192] + dot(ahead_ref[0:96, :], low)
            resid_high, resid_low = split(lines - back_ref[coil * 2 + pos])
            rows = dot(adjoint_ref[...], jnp.concatenate([resid_high, resid_low], 0))
            rows = rows + dot(low_ref[...], resid_high)
            rows_re, rows_im = rows[0:N], rows[N : 2 * N]
            grad_ref[0, pos] += coil_re * rows_re + coil_im * rows_im
            grad_ref[1, pos] += coil_re * rows_im - coil_im * rows_re
            return carry

        for side in range(2):
            coil_copy(pos, side).wait()
            lax.fori_loop(side * half, (side + 1) * half, one_coil, 0, unroll=True)
    for copy in orders:
        copy.wait()
    highs, lows = [], []
    for part in range(2):
        for pos in range(2):
            high, low = split(grad_ref[part, pos])
            highs.append(dot(depth_ref[...], high, (1, 1)).astype(BF16))
            lows.append(dot(depth_ref[...], low, (1, 1)).astype(BF16))
    total = jnp.zeros((N, 4 * N), F32)
    for channel in range(4):
        order = lane_ref[channel * N : (channel + 1) * N, :]
        total = total + dot(highs[channel], order) + dot(lows[channel], order)
    for d in range(GROUP):
        out_ref[d * GROUP : (d + 1) * GROUP, 0:VOX] = jnp.concatenate(
            [total[zz * GROUP : (zz + 1) * GROUP, d * 48 : (d + 1) * 48] for zz in range(PART)], 1
        )
    out_ref[:, VOX:WIDE] = jnp.zeros((GROUP * GROUP, WIDE - VOX), F32)


def model(images, coils, back, ahead, adjoint, low, depth_order, lane_order):
    return pl.pallas_call(
        model_kernel,
        out_shape=jax.ShapeDtypeStruct((GROUP * GROUP, WIDE), F32),
        in_specs=[VMEM, HBM, VMEM, VMEM, VMEM, VMEM, HBM, HBM],
        out_specs=VMEM,
        scratch_shapes=[
            pltpu.VMEM((2, 2, COILS, N, N), BF16),
            pltpu.VMEM((N, N), BF16),
            pltpu.VMEM((4 * N, 4 * N), BF16),
            pltpu.VMEM((2, 2, N, N), F32),
            pltpu.VMEM((2, 2, N, N), F32),
            DMA((2, 2)),
            DMA((2,)),
        ],
        compiler_params=pltpu.CompilerParams(vmem_limit_bytes=28 * MIB),
        name="model",
    )(
        images,
        in_hbm(coils),
        *map(in_vmem, (back, ahead, adjoint, low)),
        in_hbm(depth_order),
        in_hbm(lane_order),
    )


def update_kernel(grads_ref, weights_ref, pick_ref, slab_ref, out_ref):
    high, low = split(grads_ref[...].T)
    weights = weights_ref[...]
    both = dot(high, weights) + dot(low, weights)
    high, low = split(both)
    from_re = dot(pick_ref[0], high) + dot(pick_ref[0], low)
    from_im = dot(pick_ref[1], high) + dot(pick_ref[1], low)
    grad_re = from_re[:, 0:RANK] + from_im[:, RANK : 2 * RANK]
    grad_im = from_im[:, 0:RANK] - from_re[:, RANK : 2 * RANK]
    out_ref[0] = slab_ref[0] - STEP_SIZE * grad_re
    out_ref[1] = slab_ref[1] - STEP_SIZE * grad_im


def update(grads, weights, pick, slab):
    return pl.pallas_call(
        update_kernel,
        out_shape=jax.ShapeDtypeStruct((2, 2 * PART * PART, RANK), F32),
        in_specs=[VMEM] * 4,
        out_specs=VMEM,
        compiler_params=pltpu.CompilerParams(vmem_limit_bytes=16 * MIB),
        name="update",
    )(grads, weights, pick, slab)


def on_device(spatial_basis, temporal, coil_maps, kspace_data, sampled_lines):
    table = {name: jnp.asarray(value) for name, value in constants().items()}
    flat_temporal = temporal.reshape(2 * RANK, GROUP * GROUP)
    flat_basis = jnp.transpose(spatial_basis, (0, 1, 3, 2, 4)).reshape(-1, N)
    sent = frames(flat_basis, flat_temporal, table["spread"], table["inside"])
    images = lax.all_to_all(sent, "dev", 0, 0, tiled=True)
    back, ahead, adjoint, low, weights = data_back(
        kspace_data, sampled_lines, table["dft"], flat_temporal, table["frame_order"]
    )
    sent = model(
        images, coil_maps, back, ahead, adjoint, low, table["depth_order"], table["lane_order"]
    )
    grads = lax.all_to_all(
        sent.reshape(GROUP * GROUP, 1, WIDE), ("dev", "grp"), 0, 0, tiled=True
    )
    slab = lax.dynamic_slice_in_dim(spatial_basis, lax.axis_index("grp") * PART, PART, 4)
    slab = jnp.transpose(slab, (0, 3, 4, 2, 1)).reshape(2, 2 * PART * PART, RANK).astype(F32)
    result = update(grads.reshape(GROUP * GROUP, WIDE), weights, table["pick"], slab)
    return jnp.transpose(result.reshape(2, PART, PART, 2, RANK), (0, 4, 3, 1, 2))


def solution(mesh):
    placed = (
        P(None, None, None, "dev", None),
        P(),
        P(),
        P(("grp", "dev"), None, None, None, None, None),
        P(("grp", "dev"), None),
    )
    return jax.shard_map(
        on_device,
        mesh=mesh,
        in_specs=placed,
        out_specs=P(None, None, None, "dev", "grp"),
        check_vma=False,
    )
```

```python
import math

import jax
import jax.numpy as jnp
import numpy as np
from jax import lax
from jax.experimental import pallas as pl
from jax.experimental.pallas import tpu as pltpu
from jax.sharding import PartitionSpec as P

STEP_SIZE = 0.25
N = 192
PART = 12
RANK = 32
COILS = 16
LINES = 48
CHUNK = 4
GROUP = 16
VOX = 2 * PART * PART
WIDE = 384
STEPS = 8.0
TOP = 15.0
F32 = jnp.float32
BF16 = jnp.bfloat16
VMEM = pl.BlockSpec(memory_space=pltpu.VMEM)
HBM = pl.BlockSpec(memory_space=pltpu.HBM)
in_hbm = lambda array: pltpu.with_memory_space_constraint(array, pltpu.HBM)
in_vmem = lambda array: pltpu.with_memory_space_constraint(array, pltpu.VMEM)
DMA = pltpu.SemaphoreType.DMA
MIB = 1024 * 1024


def level_of(largest):
    return jnp.ceil(jnp.log2(jnp.maximum(largest, 1e-30)) * STEPS)


def scale_down(level):
    return jnp.exp2(TOP - level / STEPS)


def scale_up(level):
    return jnp.exp2(level / STEPS - TOP)


def pair_up(real, imag):
    real, imag = (
        jnp.clip(jnp.floor(part + 0.5), -32768.0, 32767.0).astype(jnp.int32)
        for part in (real, imag)
    )
    return jnp.bitwise_or(jnp.left_shift(real, 16), jnp.bitwise_and(imag, 65535))


def pair_apart(words):
    real = jnp.right_shift(words, 16)
    imag = jnp.right_shift(jnp.left_shift(words, 16), 16)
    return real.astype(F32), imag.astype(F32)


def two_terms(values):
    high = values.astype(np.float32).astype(jnp.bfloat16)
    low = (values - high.astype(np.float64)).astype(jnp.bfloat16)
    return high, low


def split(values):
    high = values.astype(BF16)
    return high, (values - high.astype(F32)).astype(BF16)


def dot(left, right, over=(1, 0)):
    return lax.dot_general(
        left, right, (((over[0],), (over[1],)), ((), ())), preferred_element_type=F32
    )


def constants():
    places = np.arange(N)
    angles = (places[:, None] * places[None, :] % N) * (2.0 * math.pi / N)
    cos_pair = two_terms(np.cos(angles) / math.sqrt(N))
    sin_pair = two_terms(np.sin(angles) / math.sqrt(N))
    dft = np.stack([*cos_pair, *sin_pair])
    columns = np.arange(2 * RANK * 2 * PART)
    spread = (columns[None, :] // (2 * PART) == np.arange(2 * RANK)[:, None])
    rows = np.arange(2 * PART)
    inside = (columns[None, :] % (2 * PART) == ((rows % PART) * 2 + rows // PART)[:, None])
    order = np.arange(N)
    depth_order = ((order % GROUP) * PART + order // GROUP)[:, None] == places[None, :]
    wide = np.arange(4 * N)
    target = (
        wide // (2 * N) * (2 * N)
        + wide // PART % GROUP * (2 * PART)
        + wide // N % 2 * PART
        + wide % PART
    )
    lane_order = target[:, None] == wide[None, :]
    peers = np.arange(GROUP * GROUP)
    frame_order = ((peers % GROUP) * GROUP + peers // GROUP)[:, None] == peers[None, :]
    out = np.arange(VOX)
    row, zz, pos = out // (2 * PART), out // 2 % PART, out % 2
    pick = (zz * 2 * PART + pos * PART + row)[:, None] == out[None, :]
    panel = np.arange(GROUP)[:, None] == np.arange(WIDE)[None, :] // (2 * PART)
    return dict(
        dft=dft,
        spread=spread.astype(jnp.bfloat16),
        inside=inside.astype(np.float32),
        depth_order=depth_order.astype(jnp.bfloat16),
        lane_order=lane_order.astype(jnp.bfloat16),
        frame_order=frame_order.astype(jnp.bfloat16),
        pick=pick.astype(jnp.bfloat16),
        panel=panel.astype(jnp.bfloat16),
    )


def frames_kernel(
    basis_ref, temporal_hbm, spread_hbm, inside_hbm, out_ref,
    temporal_ref, spread_ref, inside_ref, mix_ref, sems,
):
    copies = [
        pltpu.make_async_copy(source, target, sems.at[i])
        for i, (source, target) in enumerate(
            [(temporal_hbm, temporal_ref), (spread_hbm, spread_ref), (inside_hbm, inside_ref)]
        )
    ]
    for copy in copies:
        copy.start()
    copies[0].wait()
    first = lax.axis_index("grp") * GROUP
    frame = lax.broadcasted_iota(jnp.int32, (GROUP, GROUP * GROUP), 0) + first
    column = lax.broadcasted_iota(jnp.int32, (GROUP, GROUP * GROUP), 1)
    chosen = (frame == column).astype(F32).astype(BF16)
    weights = dot(chosen, temporal_ref[...], (1, 1))
    lane = lax.broadcasted_iota(jnp.int32, (GROUP, 2 * RANK), 1)
    from_lane = lax.broadcasted_iota(jnp.int32, (2 * RANK, 2 * RANK), 0)
    to_lane = lax.broadcasted_iota(jnp.int32, (2 * RANK, 2 * RANK), 1)
    apart = jnp.abs(from_lane - to_lane) == RANK
    swapped = dot(weights.astype(BF16), apart.astype(F32).astype(BF16))
    copies[1].wait()
    signed = jnp.where(lane < RANK, weights, -weights)
    wide_re = dot(signed.astype(BF16), spread_ref[...])
    wide_im = dot(swapped.astype(BF16), spread_ref[...])
    copies[2].wait()
    inside = inside_ref[...]
    for f in range(GROUP):
        block = jnp.concatenate(
            [inside * wide_re[f : f + 1], inside * wide_im[f : f + 1]], axis=0
        )
        mix_ref[f * 48 : (f + 1) * 48, :] = block.astype(BF16)
    images = dot(mix_ref[...], basis_ref[...])
    for f in range(GROUP):
        image = images[f * 48 : (f + 1) * 48]
        largest = jnp.max(jnp.max(jnp.abs(image), axis=0, keepdims=True), axis=1, keepdims=True)
        level = level_of(largest)
        image = image * scale_down(level)
        words = pair_up(image[0:24], image[24:48])
        words = jnp.concatenate([words[0:PART], words[PART : 2 * PART]], 1)
        for block in range(3):
            out_ref[f, block * PART : (block + 1) * PART, :] = words[
                :, block * 128 : (block + 1) * 128
            ]
        out_ref[f, 36:40, :] = jnp.broadcast_to(level, (4, 128)).astype(jnp.int32)


def frames(basis, temporal, spread, inside):
    rows = 2 * RANK * 2 * PART
    return pl.pallas_call(
        frames_kernel,
        out_shape=jax.ShapeDtypeStruct((GROUP, 40, 128), jnp.int32),
        in_specs=[VMEM, HBM, HBM, HBM],
        out_specs=VMEM,
        scratch_shapes=[
            pltpu.VMEM((2 * RANK, GROUP * GROUP), BF16),
            pltpu.VMEM((2 * RANK, rows), BF16),
            pltpu.VMEM((2 * PART, rows), F32),
            pltpu.VMEM((GROUP * 48, rows), BF16),
            DMA((3,)),
        ],
        compiler_params=pltpu.CompilerParams(vmem_limit_bytes=12 * MIB),
        name="frames",
    )(basis, *map(in_hbm, (temporal, spread, inside)))


def data_kernel(
    data_hbm, lines_hbm, dft_hbm, temporal_hbm, order_hbm,
    back_ref, ahead_ref, adjoint_ref, weights_ref,
    data_ref, lines_ref, dft_ref, temporal_ref, order_ref, data_sems, sems,
):
    small = [
        pltpu.make_async_copy(source, target, sems.at[i])
        for i, (source, target) in enumerate(
            [
                (dft_hbm, dft_ref),
                (lines_hbm, lines_ref),
                (temporal_hbm, temporal_ref),
                (order_hbm, order_ref),
            ]
        )
    ]
    chunks = [
        pltpu.make_async_copy(
            data_hbm.at[0, :, pl.ds(i * CHUNK, CHUNK)],
            data_ref.at[:, pl.ds(i * CHUNK, CHUNK)],
            data_sems.at[i],
        )
        for i in range(COILS // CHUNK)
    ]
    small[0].start()
    small[1].start()
    chunks[0].start()
    for copy in small[2:] + chunks[1:]:
        copy.start()
    small[0].wait()
    small[1].wait()
    places = lax.broadcasted_iota(jnp.int32, (N, LINES), 0)
    chosen = (places == lines_ref[...]).astype(F32)
    chosen_rows = chosen.T.astype(BF16)
    chosen = chosen.astype(BF16)
    for term in range(2):
        cos_line = dot(chosen_rows, dft_ref[term])
        sin_line = dot(chosen_rows, dft_ref[2 + term])
        from_re = jnp.concatenate([cos_line, -sin_line], 0).astype(BF16)
        from_im = jnp.concatenate([sin_line, cos_line], 0).astype(BF16)
        at = term * 96
        ahead_ref[at : at + 96, 0:N] = jnp.concatenate([cos_line, -sin_line], 0).astype(BF16)
        ahead_ref[at : at + 96, N : 2 * N] = jnp.concatenate([sin_line, cos_line], 0).astype(BF16)
        cos_back = dot(dft_ref[term], chosen)
        sin_back = dot(dft_ref[2 + term], chosen)
        adjoint_ref[0:N, at : at + 48] = cos_back.astype(BF16)
        adjoint_ref[0:N, at + 48 : at + 96] = (-sin_back).astype(BF16)
        adjoint_ref[N : 2 * N, at : at + 48] = sin_back.astype(BF16)
        adjoint_ref[N : 2 * N, at + 48 : at + 96] = cos_back.astype(BF16)

    def through(high, low, which):
        return (
            dot(high, dft_ref[which])
            + dot(low, dft_ref[which])
            + dot(high, dft_ref[which + 1])
        )

    for i in range(COILS // CHUNK):
        chunks[i].wait()
        here = slice(i * CHUNK, (i + 1) * CHUNK)
        re_high, re_low = split(data_ref[0, here].reshape(CHUNK * 2 * LINES, N))
        im_high, im_low = split(data_ref[1, here].reshape(CHUNK * 2 * LINES, N))
        back_re = through(re_high, re_low, 0) - through(im_high, im_low, 2)
        back_im = through(re_high, re_low, 2) + through(im_high, im_low, 0)
        for part, values in enumerate((back_re, back_im)):
            values = values.reshape(CHUNK, 2, LINES, N)
            at = slice(part * LINES, (part + 1) * LINES)
            for pos in range(2):
                back_ref[here, at, pos * N : (pos + 1) * N] = values[:, pos]
    small[2].wait()
    small[3].wait()
    weights = dot(order_ref[...], temporal_ref[...], (1, 1)).astype(BF16)
    peers = GROUP * GROUP
    weights_ref[0:peers, 0:RANK] = weights[:, 0:RANK]
    weights_ref[0:peers, RANK : 2 * RANK] = -weights[:, RANK : 2 * RANK]
    weights_ref[peers : 2 * peers, 0:RANK] = weights[:, RANK : 2 * RANK]
    weights_ref[peers : 2 * peers, RANK : 2 * RANK] = weights[:, 0:RANK]


def data_back(data, lines, dft, temporal, order):
    return pl.pallas_call(
        data_kernel,
        out_shape=(
            pltpu.VMEM((COILS, 2 * LINES, 2 * N), F32),
            pltpu.VMEM((4 * LINES, 2 * N), BF16),
            pltpu.VMEM((2 * N, 4 * LINES), BF16),
            jax.ShapeDtypeStruct((2 * GROUP * GROUP, 2 * RANK), BF16),
        ),
        in_specs=[HBM] * 5,
        out_specs=(VMEM,) * 4,
        scratch_shapes=[
            pltpu.VMEM((2, COILS, 2, LINES, N), F32),
            pltpu.VMEM((1, LINES), jnp.int32),
            pltpu.VMEM((4, N, N), BF16),
            pltpu.VMEM((2 * RANK, GROUP * GROUP), BF16),
            pltpu.VMEM((GROUP * GROUP, GROUP * GROUP), BF16),
            DMA((COILS // CHUNK,)),
            DMA((4,)),
        ],
        compiler_params=pltpu.CompilerParams(vmem_limit_bytes=16 * MIB),
        name="data_back",
    )(*map(in_hbm, (data, lines, dft, temporal, order)))


def model_kernel(
    images_ref, back_ref, ahead_ref, adjoint_ref, coils_hbm, depth_hbm, lane_hbm, panel_hbm,
    out_ref, coils_ref, depth_ref, lane_ref, panel_ref, field_ref, grad_ref,
    lines_ref, rows_ref, coil_sems, sems,
):
    def coil_copy(coil, part):
        return pltpu.make_async_copy(
            coils_hbm.at[part, coil], coils_ref.at[part, coil], coil_sems.at[part, coil]
        )

    for coil in range(COILS):
        for part in range(2):
            coil_copy(coil, part).start()
    orders = [
        pltpu.make_async_copy(source, target, sems.at[i])
        for i, (source, target) in enumerate(
            [(depth_hbm, depth_ref), (lane_hbm, lane_ref), (panel_hbm, panel_ref)]
        )
    ]
    for copy in orders:
        copy.start()
    for d in range(GROUP):
        here = slice(d * PART, (d + 1) * PART)
        words = images_ref[d]
        scale = scale_up(words[36:37].astype(F32))
        for part, values in enumerate(pair_apart(words[0:36])):
            values = values * scale
            for block in range(3):
                field_ref[part, here, block * 128 : (block + 1) * 128] = values[
                    block * PART : (block + 1) * PART
                ]
    grad_ref[...] = jnp.zeros_like(grad_ref)
    lines_ref[:, 0 : 2 * N] = ahead_ref[...]
    lines_ref[0:96, 2 * N : 4 * N] = ahead_ref[0:96, :]
    lines_ref[96:192, 2 * N : 4 * N] = jnp.zeros((96, 2 * N), BF16)
    rows_ref[:, 0:96] = adjoint_ref[:, 0:96]
    rows_ref[:, 96:192] = adjoint_ref[:, 0:96]
    rows_ref[:, 192:288] = adjoint_ref[:, 96:192]

    def one_coil(coil):
        coil_re, coil_im = (
            jnp.concatenate([coils_ref[part, coil, 0], coils_ref[part, coil, 1]], 1).astype(F32)
            for part in range(2)
        )
        field_re, field_im = field_ref[0], field_ref[1]
        re_high, re_low = split(coil_re * field_re - coil_im * field_im)
        im_high, im_low = split(coil_re * field_im + coil_im * field_re)
        first = dot(lines_ref[...], jnp.concatenate([re_high, im_high, re_low, im_low], 0))
        high, low = split(first[0:96] + first[96:192] - back_ref[coil])
        rows = dot(rows_ref[...], jnp.concatenate([high, low, high], 0))
        rows_re, rows_im = rows[0:N], rows[N : 2 * N]
        grad_ref[0] += coil_re * rows_re + coil_im * rows_im
        grad_ref[1] += coil_re * rows_im - coil_im * rows_re

    def some_coils(step, carry):
        for i in range(CHUNK):
            for part in range(2):
                coil_copy(step * CHUNK + i, part).wait()
        for i in range(CHUNK):
            one_coil(step * CHUNK + i)
        return carry

    lax.fori_loop(0, COILS // CHUNK, some_coils, 0)
    for copy in orders:
        copy.wait()
    total = jnp.zeros((N, 4 * N), F32)
    for channel in range(4):
        order = lane_ref[channel * N : (channel + 1) * N, :]
        for term in split(grad_ref[channel // 2, :, channel % 2 * N : (channel % 2 + 1) * N]):
            total = total + dot(dot(depth_ref[...], term, (1, 1)).astype(BF16), order)
    real = total[:, 0:WIDE].reshape(PART, GROUP, WIDE)
    imag = total[:, WIDE : 2 * WIDE].reshape(PART, GROUP, WIDE)
    largest = jnp.max(jnp.maximum(jnp.abs(real), jnp.abs(imag)), axis=0)
    largest = jnp.max(largest.T.reshape(GROUP, 2 * PART, GROUP), axis=1)
    level = level_of(largest).T
    high, low = split(level)
    level = dot(high, panel_ref[...]) + dot(low, panel_ref[...])
    scale = scale_down(level)[None]
    words = pair_up(real * scale, imag * scale)
    level = level.astype(jnp.int32)
    for d in range(GROUP):
        lanes = slice(d * 2 * PART, (d + 1) * 2 * PART)
        pieces = [words[zz, :, lanes] for zz in range(PART)]
        pieces += [level[:, lanes]] * (WIDE // (2 * PART) - PART)
        out_ref[d * GROUP : (d + 1) * GROUP, 0, :] = jnp.concatenate(pieces, 1)


def model(images, back, ahead, adjoint, coils, depth_order, lane_order, panel):
    return pl.pallas_call(
        model_kernel,
        out_shape=jax.ShapeDtypeStruct((GROUP * GROUP, 1, WIDE), jnp.int32),
        in_specs=[VMEM] * 4 + [HBM] * 4,
        out_specs=VMEM,
        scratch_shapes=[
            pltpu.VMEM((2, COILS, 2, N, N), BF16),
            pltpu.VMEM((N, N), BF16),
            pltpu.VMEM((4 * N, 4 * N), BF16),
            pltpu.VMEM((GROUP, WIDE), BF16),
            pltpu.VMEM((2, N, 2 * N), F32),
            pltpu.VMEM((2, N, 2 * N), F32),
            pltpu.VMEM((4 * LINES, 4 * N), BF16),
            pltpu.VMEM((2 * N, 6 * LINES), BF16),
            DMA((2, COILS)),
            DMA((3,)),
        ],
        compiler_params=pltpu.CompilerParams(vmem_limit_bytes=24 * MIB),
        name="model",
    )(
        images,
        *map(in_vmem, (back, ahead, adjoint)),
        *map(in_hbm, (coils, depth_order, lane_order, panel)),
    )


def update_kernel(grads_ref, weights_ref, pick_ref, slab_ref, out_ref):
    words = grads_ref[:, 0, :].T
    scale = scale_up(words[VOX : VOX + 1].astype(F32))
    real, imag = pair_apart(words[0:VOX])
    high, low = split(jnp.concatenate([real * scale, imag * scale], 1))
    grad = dot(high, weights_ref[...]) + dot(low, weights_ref[...])
    high, low = split(grad)
    grad = dot(pick_ref[...], high) + dot(pick_ref[...], low)
    out_ref[0] = slab_ref[0] - STEP_SIZE * grad[:, 0:RANK]
    out_ref[1] = slab_ref[1] - STEP_SIZE * grad[:, RANK : 2 * RANK]


def update(grads, weights, pick, slab):
    return pl.pallas_call(
        update_kernel,
        out_shape=jax.ShapeDtypeStruct((2, 2 * PART * PART, RANK), F32),
        in_specs=[VMEM] * 4,
        out_specs=VMEM,
        compiler_params=pltpu.CompilerParams(vmem_limit_bytes=16 * MIB),
        name="update",
    )(grads, weights, pick, slab)


def on_device(spatial_basis, temporal, coil_maps, kspace_data, sampled_lines):
    table = {name: jnp.asarray(value) for name, value in constants().items()}
    flat_temporal = temporal.reshape(2 * RANK, GROUP * GROUP)
    flat_basis = jnp.transpose(spatial_basis, (0, 1, 3, 2, 4)).reshape(-1, N)
    sent = frames(flat_basis, flat_temporal, table["spread"], table["inside"])
    images = lax.all_to_all(sent, "dev", 0, 0, tiled=True)
    back, ahead, adjoint, weights = data_back(
        kspace_data, sampled_lines, table["dft"], flat_temporal, table["frame_order"]
    )
    sent = model(
        images, back, ahead, adjoint, coil_maps,
        table["depth_order"], table["lane_order"], table["panel"],
    )
    grads = lax.all_to_all(sent, ("dev", "grp"), 0, 0, tiled=True)
    slab = lax.dynamic_slice_in_dim(spatial_basis, lax.axis_index("grp") * PART, PART, 4)
    slab = jnp.transpose(slab, (0, 3, 4, 2, 1)).reshape(2, 2 * PART * PART, RANK).astype(F32)
    result = update(grads, weights, table["pick"], slab)
    return jnp.transpose(result.reshape(2, PART, PART, 2, RANK), (0, 4, 3, 1, 2))


def solution(mesh):
    placed = (
        P(None, None, None, "dev", None),
        P(),
        P(),
        P(("grp", "dev"), None, None, None, None, None),
        P(("grp", "dev"), None),
    )
    return jax.shard_map(
        on_device,
        mesh=mesh,
        in_specs=placed,
        out_specs=P(None, None, None, "dev", "grp"),
        check_vma=False,
    )
```

```python
import functools
import math

import jax
import jax.numpy as jnp
import numpy as np
from jax import lax
from jax.experimental import pallas as pl
from jax.experimental.pallas import tpu as pltpu
from jax.sharding import PartitionSpec as P

STEP_SIZE = 0.25
N = 192
PART = 12
RANK = 32
COILS = 16
LINES = 48
EARLY = 1
GROUPS = [range(1, 3), range(3, 6), range(6, 11), range(11, 16)]
CHUNK = 4
TOGETHER = 15
GROUP = 16
VOX = 2 * PART * PART
WIDE = 384
STEPS = 8.0
TOP = 15.0
F32 = jnp.float32
BF16 = jnp.bfloat16
VMEM = pl.BlockSpec(memory_space=pltpu.VMEM)
HBM = pl.BlockSpec(memory_space=pltpu.HBM)
in_hbm = lambda array: pltpu.with_memory_space_constraint(array, pltpu.HBM)
in_vmem = lambda array: pltpu.with_memory_space_constraint(array, pltpu.VMEM)
DMA = pltpu.SemaphoreType.DMA
MIB = 1024 * 1024


def level_of(largest):
    return jnp.ceil(jnp.log2(jnp.maximum(largest, 1e-30)) * STEPS)


def scale_down(level):
    return jnp.exp2(TOP - level / STEPS)


def scale_up(level):
    return jnp.exp2(level / STEPS - TOP)


def pair_up(real, imag):
    real, imag = (
        jnp.clip(jnp.floor(part + 0.5), -32768.0, 32767.0).astype(jnp.int32)
        for part in (real, imag)
    )
    return jnp.bitwise_or(jnp.left_shift(real, 16), jnp.bitwise_and(imag, 65535))


def pair_apart(words):
    real = jnp.right_shift(words, 16)
    imag = jnp.right_shift(jnp.left_shift(words, 16), 16)
    return real.astype(F32), imag.astype(F32)


def two_terms(values):
    high = values.astype(np.float32).astype(jnp.bfloat16)
    low = (values - high.astype(np.float64)).astype(jnp.bfloat16)
    return high, low


def split(values):
    high = values.astype(BF16)
    return high, (values - high.astype(F32)).astype(BF16)


def dot(left, right, over=(1, 0)):
    return lax.dot_general(
        left, right, (((over[0],), (over[1],)), ((), ())), preferred_element_type=F32
    )


def constants():
    places = np.arange(N)
    angles = (places[:, None] * places[None, :] % N) * (2.0 * math.pi / N)
    cos_pair = two_terms(np.cos(angles) / math.sqrt(N))
    sin_pair = two_terms(np.sin(angles) / math.sqrt(N))
    dft = np.stack([*cos_pair, *sin_pair])
    columns = np.arange(2 * RANK * 2 * PART)
    spread = (columns[None, :] // (2 * PART) == np.arange(2 * RANK)[:, None])
    rows = np.arange(2 * PART)
    inside = (columns[None, :] % (2 * PART) == ((rows % PART) * 2 + rows // PART)[:, None])
    order = np.arange(N)
    depth_order = ((order % GROUP) * PART + order // GROUP)[:, None] == places[None, :]
    peers = np.arange(GROUP * GROUP)
    frame_order = ((peers % GROUP) * GROUP + peers // GROUP)[:, None] == peers[None, :]
    out = np.arange(VOX)
    row, zz, pos = out // (2 * PART), out // 2 % PART, out % 2
    pick = (zz * 2 * PART + pos * PART + row)[:, None] == out[None, :]
    panel = places[:, None] == places[None, :] // PART * PART
    return dict(
        dft=dft,
        spread=spread.astype(jnp.bfloat16),
        inside=inside.astype(np.float32),
        depth_order=depth_order.astype(jnp.bfloat16),
        frame_order=frame_order.astype(jnp.bfloat16),
        pick=pick.astype(jnp.bfloat16),
        panel=panel.astype(jnp.bfloat16),
    )


def frames_kernel(
    basis_hbm, temporal_hbm, spread_hbm, inside_hbm, out_ref,
    basis_ref, temporal_ref, spread_ref, inside_ref, mix_ref, sems,
):
    copies = [
        pltpu.make_async_copy(source, target, sems.at[i])
        for i, (source, target) in enumerate(
            [
                (temporal_hbm, temporal_ref),
                (spread_hbm, spread_ref),
                (inside_hbm, inside_ref),
                (basis_hbm, basis_ref),
            ]
        )
    ]
    for copy in copies:
        copy.start()
    copies[0].wait()
    first = lax.axis_index("grp") * GROUP
    frame = lax.broadcasted_iota(jnp.int32, (GROUP, GROUP * GROUP), 0) + first
    column = lax.broadcasted_iota(jnp.int32, (GROUP, GROUP * GROUP), 1)
    chosen = (frame == column).astype(F32).astype(BF16)
    weights = dot(chosen, temporal_ref[...], (1, 1))
    lane = lax.broadcasted_iota(jnp.int32, (GROUP, 2 * RANK), 1)
    from_lane = lax.broadcasted_iota(jnp.int32, (2 * RANK, 2 * RANK), 0)
    to_lane = lax.broadcasted_iota(jnp.int32, (2 * RANK, 2 * RANK), 1)
    apart = jnp.abs(from_lane - to_lane) == RANK
    swapped = dot(weights.astype(BF16), apart.astype(F32).astype(BF16))
    copies[1].wait()
    signed = jnp.where(lane < RANK, weights, -weights)
    wide_re = dot(signed.astype(BF16), spread_ref[...])
    wide_im = dot(swapped.astype(BF16), spread_ref[...])
    copies[2].wait()
    inside = inside_ref[...]
    for f in range(GROUP):
        block = jnp.concatenate(
            [inside * wide_re[f : f + 1], inside * wide_im[f : f + 1]], axis=0
        )
        mix_ref[f * 48 : (f + 1) * 48, :] = block.astype(BF16)
    copies[3].wait()
    basis = basis_ref[...].reshape(2 * RANK * 2 * PART, N)
    images = dot(mix_ref[...], basis)
    for f in range(GROUP):
        image = images[f * 48 : (f + 1) * 48]
        largest = jnp.max(jnp.max(jnp.abs(image), axis=0, keepdims=True), axis=1, keepdims=True)
        level = level_of(largest)
        image = image * scale_down(level)
        words = pair_up(image[0:24], image[24:48])
        words = jnp.concatenate([words[0:PART], words[PART : 2 * PART]], 1)
        for block in range(3):
            out_ref[f, block * PART : (block + 1) * PART, :] = words[
                :, block * 128 : (block + 1) * 128
            ]
        out_ref[f, 36:40, :] = jnp.broadcast_to(level, (4, 128)).astype(jnp.int32)


def frames(basis, temporal, spread, inside):
    rows = 2 * RANK * 2 * PART
    return pl.pallas_call(
        frames_kernel,
        out_shape=jax.ShapeDtypeStruct((GROUP, 40, 128), jnp.int32),
        in_specs=[HBM] * 4,
        out_specs=VMEM,
        scratch_shapes=[
            pltpu.VMEM((rows // 2, 2, N), BF16),
            pltpu.VMEM((2 * RANK, GROUP * GROUP), BF16),
            pltpu.VMEM((2 * RANK, rows), BF16),
            pltpu.VMEM((2 * PART, rows), F32),
            pltpu.VMEM((GROUP * 48, rows), BF16),
            DMA((4,)),
        ],
        compiler_params=pltpu.CompilerParams(vmem_limit_bytes=16 * MIB),
        name="frames",
    )(*map(in_hbm, (basis, temporal, spread, inside)))


def data_kernel(
    data_hbm, coils_hbm, lines_hbm, dft_hbm, temporal_hbm, order_hbm,
    back_ref, early_ref, ahead_ref, adjoint_ref, weights_ref,
    data_ref, lines_ref, dft_ref, temporal_ref, order_ref, data_sems, sems,
):
    small = [
        pltpu.make_async_copy(source, target, sems.at[i])
        for i, (source, target) in enumerate(
            [
                (dft_hbm, dft_ref),
                (lines_hbm, lines_ref),
                (temporal_hbm, temporal_ref),
                (order_hbm, order_ref),
                (coils_hbm.at[:, pl.ds(0, EARLY)], early_ref),
            ]
        )
    ]
    chunks = [
        pltpu.make_async_copy(
            data_hbm.at[0, :, pl.ds(i * CHUNK, CHUNK)],
            data_ref.at[:, pl.ds(i * CHUNK, CHUNK)],
            data_sems.at[i],
        )
        for i in range(COILS // CHUNK)
    ]
    small[0].start()
    small[1].start()
    chunks[0].start()
    for copy in small[2:] + chunks[1:]:
        copy.start()
    small[0].wait()
    small[1].wait()
    places = lax.broadcasted_iota(jnp.int32, (N, LINES), 0)
    chosen = (places == lines_ref[...]).astype(F32)
    chosen_rows = chosen.T.astype(BF16)
    chosen = chosen.astype(BF16)
    for term in range(2):
        cos_line = dot(chosen_rows, dft_ref[term])
        sin_line = dot(chosen_rows, dft_ref[2 + term])
        from_re = jnp.concatenate([cos_line, -sin_line], 0).astype(BF16)
        from_im = jnp.concatenate([sin_line, cos_line], 0).astype(BF16)
        at = term * 96
        ahead_ref[at : at + 96, 0:N] = jnp.concatenate([cos_line, -sin_line], 0).astype(BF16)
        ahead_ref[at : at + 96, N : 2 * N] = jnp.concatenate([sin_line, cos_line], 0).astype(BF16)
        cos_back = dot(dft_ref[term], chosen)
        sin_back = dot(dft_ref[2 + term], chosen)
        adjoint_ref[0:N, at : at + 48] = cos_back.astype(BF16)
        adjoint_ref[0:N, at + 48 : at + 96] = (-sin_back).astype(BF16)
        adjoint_ref[N : 2 * N, at : at + 48] = sin_back.astype(BF16)
        adjoint_ref[N : 2 * N, at + 48 : at + 96] = cos_back.astype(BF16)

    def through(high, low, which):
        return (
            dot(high, dft_ref[which])
            + dot(low, dft_ref[which])
            + dot(high, dft_ref[which + 1])
        )

    for i in range(COILS // CHUNK):
        chunks[i].wait()
        here = slice(i * CHUNK, (i + 1) * CHUNK)
        re_high, re_low = split(data_ref[0, here].reshape(CHUNK * 2 * LINES, N))
        im_high, im_low = split(data_ref[1, here].reshape(CHUNK * 2 * LINES, N))
        back_re = through(re_high, re_low, 0) - through(im_high, im_low, 2)
        back_im = through(re_high, re_low, 2) + through(im_high, im_low, 0)
        for part, values in enumerate((back_re, back_im)):
            values = values.reshape(CHUNK, 2, LINES, N)
            at = slice(part * LINES, (part + 1) * LINES)
            for pos in range(2):
                back_ref[here, at, pos * N : (pos + 1) * N] = values[:, pos]
    small[2].wait()
    small[3].wait()
    small[4].wait()
    weights = dot(order_ref[...], temporal_ref[...], (1, 1)).astype(BF16)
    peers = GROUP * GROUP
    weights_ref[0:peers, 0:RANK] = weights[:, 0:RANK]
    weights_ref[0:peers, RANK : 2 * RANK] = -weights[:, RANK : 2 * RANK]
    weights_ref[peers : 2 * peers, 0:RANK] = weights[:, RANK : 2 * RANK]
    weights_ref[peers : 2 * peers, RANK : 2 * RANK] = weights[:, 0:RANK]


def data_back(data, coils, lines, dft, temporal, order):
    return pl.pallas_call(
        data_kernel,
        out_shape=(
            pltpu.VMEM((COILS, 2 * LINES, 2 * N), F32),
            pltpu.VMEM((2, EARLY, 2, N, N), BF16),
            pltpu.VMEM((4 * LINES, 2 * N), BF16),
            pltpu.VMEM((2 * N, 4 * LINES), BF16),
            jax.ShapeDtypeStruct((2 * GROUP * GROUP, 2 * RANK), BF16),
        ),
        in_specs=[HBM] * 6,
        out_specs=(VMEM,) * 5,
        scratch_shapes=[
            pltpu.VMEM((2, COILS, 2, LINES, N), F32),
            pltpu.VMEM((1, LINES), jnp.int32),
            pltpu.VMEM((4, N, N), BF16),
            pltpu.VMEM((2 * RANK, GROUP * GROUP), BF16),
            pltpu.VMEM((GROUP * GROUP, GROUP * GROUP), BF16),
            DMA((COILS // CHUNK,)),
            DMA((5,)),
        ],
        compiler_params=pltpu.CompilerParams(vmem_limit_bytes=16 * MIB),
        name="data_back",
    )(*map(in_hbm, (data, coils, lines, dft, temporal, order)))


def model_kernel(
    images_ref, back_ref, early_ref, ahead_ref, adjoint_ref, coils_hbm, depth_hbm, panel_hbm,
    out_ref, coils_ref, depth_ref, panel_ref, field_ref, grad_ref,
    lines_ref, rows_ref, resid_ref, coil_sems, sems,
):
    def coil_copy(coil, part):
        return pltpu.make_async_copy(
            coils_hbm.at[part, coil], coils_ref.at[part, coil], coil_sems.at[part, coil]
        )

    def coil_group(group):
        return [coil_copy(coil, part) for coil in GROUPS[group] for part in range(2)]

    for group in range(2):
        for copy in coil_group(group):
            copy.start()
    orders = [
        pltpu.make_async_copy(source, target, sems.at[i])
        for i, (source, target) in enumerate(
            [(depth_hbm, depth_ref), (panel_hbm, panel_ref)]
        )
    ]
    for copy in orders:
        copy.start()
    for d in range(GROUP):
        here = slice(d * PART, (d + 1) * PART)
        words = images_ref[d]
        scale = scale_up(words[36:37].astype(F32))
        for part, values in enumerate(pair_apart(words[0:36])):
            values = values * scale
            for block in range(3):
                field_ref[part, here, block * 128 : (block + 1) * 128] = values[
                    block * PART : (block + 1) * PART
                ]
    lines_ref[:, 0 : 2 * N] = ahead_ref[...]
    lines_ref[0:96, 2 * N : 4 * N] = ahead_ref[0:96, :]
    lines_ref[96:192, 2 * N : 4 * N] = jnp.zeros((96, 2 * N), BF16)
    rows_ref[:, 0:96] = adjoint_ref[:, 0:96]
    rows_ref[:, 96:192] = adjoint_ref[:, 0:96]
    rows_ref[:, 192:288] = adjoint_ref[:, 96:192]

    def coil_pair(coil, source):
        return (
            jnp.concatenate([source[part, coil, 0], source[part, coil, 1]], 1).astype(F32)
            for part in range(2)
        )

    def ahead_one(coil, source):
        coil_re, coil_im = coil_pair(coil, source)
        field_re, field_im = field_ref[0], field_ref[1]
        re_high, re_low = split(coil_re * field_re - coil_im * field_im)
        im_high, im_low = split(coil_re * field_im + coil_im * field_re)
        first = dot(lines_ref[...], jnp.concatenate([re_high, im_high, re_low, im_low], 0))
        high, low = split(first[0:96] + first[96:192] - back_ref[coil])
        resid_ref[coil, 0:96] = high
        resid_ref[coil, 96:192] = low
        resid_ref[coil, 192:288] = high

    def back_one(coil, source):
        coil_re, coil_im = coil_pair(coil, source)
        rows = dot(rows_ref[...], resid_ref[coil])
        rows_re, rows_im = rows[0:N], rows[N : 2 * N]
        return coil_re * rows_re + coil_im * rows_im, coil_re * rows_im - coil_im * rows_re

    for coil in range(EARLY):
        ahead_one(coil, early_ref)
    for group, coils in enumerate(GROUPS):
        for copy in coil_group(group):
            copy.wait()
        if group + 2 < len(GROUPS):
            for copy in coil_group(group + 2):
                copy.start()
        for coil in coils:
            ahead_one(coil, coils_ref)
    for coil in range(EARLY):
        grad_ref[0], grad_ref[1] = back_one(coil, early_ref)

    def some_back(step, carry):
        for i in range(TOGETHER):
            grad_re, grad_im = back_one(EARLY + step * TOGETHER + i, coils_ref)
            grad_ref[0] += grad_re
            grad_ref[1] += grad_im
        return carry

    lax.fori_loop(0, (COILS - EARLY) // TOGETHER, some_back, 0)
    for copy in orders:
        copy.wait()
    parts = []
    for part in range(2):
        for pos in range(2):
            high, low = split(grad_ref[part, :, pos * N : (pos + 1) * N])
            moved = dot(depth_ref[...], high, (1, 1)) + dot(depth_ref[...], low, (1, 1))
            parts.append(moved.reshape(PART, GROUP, N))
    largest = functools.reduce(jnp.maximum, map(jnp.abs, parts))
    largest = jnp.max(largest, axis=0)
    for shift in (1, 2, 4, 4):
        ahead = jnp.concatenate([largest[:, shift:], largest[:, :shift]], 1)
        largest = jnp.maximum(largest, ahead)
    high, low = split(level_of(largest))
    level = dot(high, panel_ref[...]) + dot(low, panel_ref[...])
    scale = scale_down(level)[None]
    words = [pair_up(parts[pos] * scale, parts[2 + pos] * scale) for pos in range(2)]
    level = level.astype(jnp.int32)
    for d in range(GROUP):
        lanes = slice(d * PART, (d + 1) * PART)
        pieces = [words[pos][zz, :, lanes] for zz in range(PART) for pos in range(2)]
        pieces.append(jnp.broadcast_to(level[:, d * PART : d * PART + 1], (GROUP, WIDE - VOX)))
        out_ref[d * GROUP : (d + 1) * GROUP, 0, :] = jnp.concatenate(pieces, 1)


def model(images, back, early, ahead, adjoint, coils, depth_order, panel):
    return pl.pallas_call(
        model_kernel,
        out_shape=jax.ShapeDtypeStruct((GROUP * GROUP, 1, WIDE), jnp.int32),
        in_specs=[VMEM] * 5 + [HBM] * 3,
        out_specs=VMEM,
        scratch_shapes=[
            pltpu.VMEM((2, COILS, 2, N, N), BF16),
            pltpu.VMEM((N, N), BF16),
            pltpu.VMEM((N, N), BF16),
            pltpu.VMEM((2, N, 2 * N), F32),
            pltpu.VMEM((2, N, 2 * N), F32),
            pltpu.VMEM((4 * LINES, 4 * N), BF16),
            pltpu.VMEM((2 * N, 6 * LINES), BF16),
            pltpu.VMEM((COILS, 6 * LINES, 2 * N), BF16),
            DMA((2, COILS)),
            DMA((2,)),
        ],
        compiler_params=pltpu.CompilerParams(vmem_limit_bytes=32 * MIB),
        name="model",
    )(
        images,
        *map(in_vmem, (back, early, ahead, adjoint)),
        *map(in_hbm, (coils, depth_order, panel)),
    )


def update_kernel(grads_ref, weights_ref, pick_ref, slab_ref, out_ref):
    words = grads_ref[:, 0, :].T
    scale = scale_up(words[VOX : VOX + 1].astype(F32))
    real, imag = pair_apart(words[0:VOX])
    high, low = split(jnp.concatenate([real * scale, imag * scale], 1))
    grad = dot(high, weights_ref[...]) + dot(low, weights_ref[...])
    high, low = split(grad)
    grad = dot(pick_ref[...], high) + dot(pick_ref[...], low)
    out_ref[0] = slab_ref[0] - STEP_SIZE * grad[:, 0:RANK]
    out_ref[1] = slab_ref[1] - STEP_SIZE * grad[:, RANK : 2 * RANK]


def update(grads, weights, pick, slab):
    return pl.pallas_call(
        update_kernel,
        out_shape=jax.ShapeDtypeStruct((2, 2 * PART * PART, RANK), F32),
        in_specs=[VMEM] * 4,
        out_specs=VMEM,
        compiler_params=pltpu.CompilerParams(vmem_limit_bytes=16 * MIB),
        name="update",
    )(grads, weights, pick, slab)


def on_device(spatial_basis, temporal, coil_maps, kspace_data, sampled_lines):
    table = {name: jnp.asarray(value) for name, value in constants().items()}
    flat_temporal = temporal.reshape(2 * RANK, GROUP * GROUP)
    flat_basis = jnp.transpose(spatial_basis, (0, 1, 3, 2, 4)).reshape(-1, 2, N)
    sent = frames(flat_basis, flat_temporal, table["spread"], table["inside"])
    images = lax.all_to_all(sent, "dev", 0, 0, tiled=True)
    back, early, ahead, adjoint, weights = data_back(
        kspace_data, coil_maps, sampled_lines, table["dft"], flat_temporal, table["frame_order"]
    )
    sent = model(
        images, back, early, ahead, adjoint, coil_maps, table["depth_order"], table["panel"]
    )
    grads = lax.all_to_all(sent, ("dev", "grp"), 0, 0, tiled=True)
    slab = lax.dynamic_slice_in_dim(spatial_basis, lax.axis_index("grp") * PART, PART, 4)
    slab = jnp.transpose(slab, (0, 3, 4, 2, 1)).reshape(2, 2 * PART * PART, RANK).astype(F32)
    result = update(grads, weights, table["pick"], slab)
    return jnp.transpose(result.reshape(2, PART, PART, 2, RANK), (0, 4, 3, 1, 2))


def solution(mesh):
    placed = (
        P(None, None, None, "dev", None),
        P(),
        P(),
        P(("grp", "dev"), None, None, None, None, None),
        P(("grp", "dev"), None),
    )
    return jax.shard_map(
        on_device,
        mesh=mesh,
        in_specs=placed,
        out_specs=P(None, None, None, "dev", "grp"),
        check_vma=False,
    )
```

```python
import functools
import math

import jax
import jax.numpy as jnp
import numpy as np
from jax import lax
from jax.experimental import pallas as pl
from jax.experimental.pallas import tpu as pltpu
from jax.sharding import PartitionSpec as P

STEP_SIZE = 0.25
N = 192
PART = 12
ROWS = 4
RANK = 32
COILS = 16
LINES = 48
EARLY = 1
GROUPS = [[(0,)], [(1, 2)], [(3, 4), (5, 6)], [(7, 8), (9, 10)], [(11, 12), (13, 14), (15,)]]
CHUNK = 4
GROUP = 16
VOX = 2 * PART * PART
WIDE = 384
STEPS = 8.0
TOP = 15.0
F32 = jnp.float32
BF16 = jnp.bfloat16
VMEM = pl.BlockSpec(memory_space=pltpu.VMEM)
HBM = pl.BlockSpec(memory_space=pltpu.HBM)
in_hbm = lambda array: pltpu.with_memory_space_constraint(array, pltpu.HBM)
in_vmem = lambda array: pltpu.with_memory_space_constraint(array, pltpu.VMEM)
DMA = pltpu.SemaphoreType.DMA
MIB = 1024 * 1024


def level_of(largest):
    return jnp.ceil(jnp.log2(jnp.maximum(largest, 1e-30)) * STEPS)


def scale_down(level):
    return jnp.exp2(TOP - level / STEPS)


def scale_up(level):
    return jnp.exp2(level / STEPS - TOP)


def pair_up(real, imag):
    real, imag = (
        jnp.clip(jnp.floor(part + 0.5), -32768.0, 32767.0).astype(jnp.int32)
        for part in (real, imag)
    )
    return jnp.bitwise_or(jnp.left_shift(real, 16), jnp.bitwise_and(imag, 65535))


def pair_apart(words):
    real = jnp.right_shift(words, 16)
    imag = jnp.right_shift(jnp.left_shift(words, 16), 16)
    return real.astype(F32), imag.astype(F32)


def two_terms(values):
    high = values.astype(np.float32).astype(jnp.bfloat16)
    low = (values - high.astype(np.float64)).astype(jnp.bfloat16)
    return high, low


def split(values):
    high = values.astype(BF16)
    return high, (values - high.astype(F32)).astype(BF16)


def dot(left, right, over=(1, 0)):
    return lax.dot_general(
        left, right, (((over[0],), (over[1],)), ((), ())), preferred_element_type=F32
    )


def constants():
    places = np.arange(N)
    angles = (places[:, None] * places[None, :] % N) * (2.0 * math.pi / N)
    cos_pair = two_terms(np.cos(angles) / math.sqrt(N))
    sin_pair = two_terms(np.sin(angles) / math.sqrt(N))
    dft = np.stack([*cos_pair, *sin_pair])
    columns = np.arange(2 * RANK * 2 * ROWS)
    spread = columns[None, :] // (2 * ROWS) == np.arange(2 * RANK)[:, None]
    rows = np.arange(2 * ROWS)
    inside = columns[None, :] % (2 * ROWS) == ((rows % ROWS) * 2 + rows // ROWS)[:, None]
    order = np.arange(N)
    depth_order = ((order % GROUP) * PART + order // GROUP)[:, None] == places[None, :]
    peers = np.arange(GROUP * GROUP)
    frame_order = ((peers % GROUP) * GROUP + peers // GROUP)[:, None] == peers[None, :]
    out = np.arange(VOX)
    row, zz, pos = out // (2 * PART), out // 2 % PART, out % 2
    pick = (zz * 2 * PART + pos * PART + row)[:, None] == out[None, :]
    panel = places[:, None] == places[None, :] // PART * PART
    return dict(
        dft=dft,
        spread=spread.astype(jnp.bfloat16),
        inside=inside.astype(np.float32),
        depth_order=depth_order.astype(jnp.bfloat16),
        frame_order=frame_order.astype(jnp.bfloat16),
        pick=pick.astype(jnp.bfloat16),
        panel=panel.astype(jnp.bfloat16),
    )


def frames_kernel(
    basis_hbm, temporal_hbm, spread_hbm, inside_hbm, out_ref,
    basis_ref, temporal_ref, spread_ref, inside_ref, mix_ref, basis_sem, sems,
):
    copies = [
        pltpu.make_async_copy(source, target, sems.at[i])
        for i, (source, target) in enumerate(
            [
                (temporal_hbm, temporal_ref),
                (spread_hbm, spread_ref),
                (inside_hbm, inside_ref),
            ]
        )
    ]
    whole = pltpu.make_async_copy(basis_hbm, basis_ref, basis_sem)
    whole.start()
    for copy in copies:
        copy.start()
    copies[0].wait()
    first = lax.axis_index("grp") * GROUP
    frame = lax.broadcasted_iota(jnp.int32, (GROUP, GROUP * GROUP), 0) + first
    column = lax.broadcasted_iota(jnp.int32, (GROUP, GROUP * GROUP), 1)
    chosen = (frame == column).astype(F32).astype(BF16)
    weights = dot(chosen, temporal_ref[...], (1, 1))
    lane = lax.broadcasted_iota(jnp.int32, (GROUP, 2 * RANK), 1)
    from_lane = lax.broadcasted_iota(jnp.int32, (2 * RANK, 2 * RANK), 0)
    to_lane = lax.broadcasted_iota(jnp.int32, (2 * RANK, 2 * RANK), 1)
    apart = jnp.abs(from_lane - to_lane) == RANK
    swapped = dot(weights.astype(BF16), apart.astype(F32).astype(BF16))
    copies[1].wait()
    signed = jnp.where(lane < RANK, weights, -weights)
    wide_re = dot(signed.astype(BF16), spread_ref[...])
    wide_im = dot(swapped.astype(BF16), spread_ref[...])
    copies[2].wait()
    inside = inside_ref[...]
    wide = jnp.concatenate([wide_re[:, None], wide_im[:, None]], 1)
    mix = inside[None, None] * wide[:, :, None]
    mix_ref[...] = mix.reshape(2 * GROUP * 2 * ROWS, wide_re.shape[1]).astype(BF16)
    images = []
    whole.wait()
    for i in range(PART // ROWS):
        basis = basis_ref[:, i * ROWS : (i + 1) * ROWS].reshape(2 * RANK * 2 * ROWS, N)
        images.append(dot(mix_ref[...], basis).reshape(GROUP, 2, 2 * ROWS, N))
    largest = functools.reduce(jnp.maximum, [jnp.max(jnp.abs(image), axis=1) for image in images])
    largest = jnp.max(jnp.max(largest, axis=1, keepdims=True), axis=2, keepdims=True)
    level = level_of(largest)
    scale = scale_down(level)
    for i, image in enumerate(images):
        words = pair_up(image[:, 0] * scale, image[:, 1] * scale)
        words = jnp.concatenate([words[:, 0:ROWS], words[:, ROWS : 2 * ROWS]], 2)
        for block in range(3):
            at = block * PART + i * ROWS
            out_ref[:, at : at + ROWS, :] = words[:, :, block * 128 : (block + 1) * 128]
    out_ref[:, 36:40, :] = jnp.broadcast_to(level, (GROUP, 4, 128)).astype(jnp.int32)


def frames(basis, temporal, spread, inside):
    rows = 2 * RANK * 2 * ROWS
    return pl.pallas_call(
        frames_kernel,
        out_shape=jax.ShapeDtypeStruct((GROUP, 40, 128), jnp.int32),
        in_specs=[HBM] * 4,
        out_specs=VMEM,
        scratch_shapes=[
            pltpu.VMEM((2 * RANK, PART, 2, N), BF16),
            pltpu.VMEM((2 * RANK, GROUP * GROUP), BF16),
            pltpu.VMEM((2 * RANK, rows), BF16),
            pltpu.VMEM((2 * ROWS, rows), F32),
            pltpu.VMEM((2 * GROUP * 2 * ROWS, rows), BF16),
            DMA(()),
            DMA((3,)),
        ],
        compiler_params=pltpu.CompilerParams(vmem_limit_bytes=16 * MIB),
        name="frames",
    )(*map(in_hbm, (basis, temporal, spread, inside)))


def data_kernel(
    data_hbm, coils_hbm, lines_hbm, dft_hbm, temporal_hbm, order_hbm,
    back_ref, early_ref, ahead_ref, adjoint_ref, weights_ref,
    data_ref, lines_ref, dft_ref, temporal_ref, order_ref, data_sems, sems,
):
    small = [
        pltpu.make_async_copy(source, target, sems.at[i])
        for i, (source, target) in enumerate(
            [
                (dft_hbm, dft_ref),
                (lines_hbm, lines_ref),
                (temporal_hbm, temporal_ref),
                (order_hbm, order_ref),
                (coils_hbm.at[:, pl.ds(0, EARLY)], early_ref),
            ]
        )
    ]
    chunks = [
        pltpu.make_async_copy(
            data_hbm.at[0, :, pl.ds(i * CHUNK, CHUNK)],
            data_ref.at[:, pl.ds(i * CHUNK, CHUNK)],
            data_sems.at[i],
        )
        for i in range(COILS // CHUNK)
    ]
    small[0].start()
    small[1].start()
    chunks[0].start()
    for copy in small[2:] + chunks[1:]:
        copy.start()
    small[0].wait()
    small[1].wait()
    places = lax.broadcasted_iota(jnp.int32, (N, LINES), 0)
    chosen = (places == lines_ref[...]).astype(F32)
    chosen_rows = chosen.T.astype(BF16)
    chosen = chosen.astype(BF16)
    for term in range(2):
        cos_line = dot(chosen_rows, dft_ref[term])
        sin_line = dot(chosen_rows, dft_ref[2 + term])
        from_re = jnp.concatenate([cos_line, -sin_line], 0).astype(BF16)
        from_im = jnp.concatenate([sin_line, cos_line], 0).astype(BF16)
        at = term * 96
        ahead_ref[at : at + 96, 0:N] = jnp.concatenate([cos_line, -sin_line], 0).astype(BF16)
        ahead_ref[at : at + 96, N : 2 * N] = jnp.concatenate([sin_line, cos_line], 0).astype(BF16)
        cos_back = dot(dft_ref[term], chosen)
        sin_back = dot(dft_ref[2 + term], chosen)
        adjoint_ref[0:N, at : at + 48] = cos_back.astype(BF16)
        adjoint_ref[0:N, at + 48 : at + 96] = (-sin_back).astype(BF16)
        adjoint_ref[N : 2 * N, at : at + 48] = sin_back.astype(BF16)
        adjoint_ref[N : 2 * N, at + 48 : at + 96] = cos_back.astype(BF16)

    def through(high, low, which):
        return (
            dot(high, dft_ref[which])
            + dot(low, dft_ref[which])
            + dot(high, dft_ref[which + 1])
        )

    for i in range(COILS // CHUNK):
        chunks[i].wait()
        here = slice(i * CHUNK, (i + 1) * CHUNK)
        re_high, re_low = split(data_ref[0, here].reshape(CHUNK * 2 * LINES, N))
        im_high, im_low = split(data_ref[1, here].reshape(CHUNK * 2 * LINES, N))
        back_re = through(re_high, re_low, 0) - through(im_high, im_low, 2)
        back_im = through(re_high, re_low, 2) + through(im_high, im_low, 0)
        for part, values in enumerate((back_re, back_im)):
            values = values.reshape(CHUNK, 2, LINES, N)
            at = slice(part * LINES, (part + 1) * LINES)
            for pos in range(2):
                back_ref[here, at, pos * N : (pos + 1) * N] = values[:, pos]
    small[2].wait()
    small[3].wait()
    small[4].wait()
    weights = dot(order_ref[...], temporal_ref[...], (1, 1)).astype(BF16)
    peers = GROUP * GROUP
    weights_ref[0:peers, 0:RANK] = weights[:, 0:RANK]
    weights_ref[0:peers, RANK : 2 * RANK] = -weights[:, RANK : 2 * RANK]
    weights_ref[peers : 2 * peers, 0:RANK] = weights[:, RANK : 2 * RANK]
    weights_ref[peers : 2 * peers, RANK : 2 * RANK] = weights[:, 0:RANK]


def data_back(data, coils, lines, dft, temporal, order):
    return pl.pallas_call(
        data_kernel,
        out_shape=(
            pltpu.VMEM((COILS, 2 * LINES, 2 * N), F32),
            pltpu.VMEM((2, EARLY, 2, N, N), BF16),
            pltpu.VMEM((4 * LINES, 2 * N), BF16),
            pltpu.VMEM((2 * N, 4 * LINES), BF16),
            jax.ShapeDtypeStruct((2 * GROUP * GROUP, 2 * RANK), BF16),
        ),
        in_specs=[HBM] * 6,
        out_specs=(VMEM,) * 5,
        scratch_shapes=[
            pltpu.VMEM((2, COILS, 2, LINES, N), F32),
            pltpu.VMEM((1, LINES), jnp.int32),
            pltpu.VMEM((4, N, N), BF16),
            pltpu.VMEM((2 * RANK, GROUP * GROUP), BF16),
            pltpu.VMEM((GROUP * GROUP, GROUP * GROUP), BF16),
            DMA((COILS // CHUNK,)),
            DMA((5,)),
        ],
        compiler_params=pltpu.CompilerParams(vmem_limit_bytes=16 * MIB),
        name="data_back",
    )(*map(in_hbm, (data, coils, lines, dft, temporal, order)))


def model_kernel(
    images_ref, back_ref, early_ref, ahead_ref, adjoint_ref, coils_hbm, depth_hbm, panel_hbm,
    out_ref, coils_ref, depth_ref, panel_ref, field_ref, grad_ref,
    lines_ref, rows_ref, resid_ref, coil_sems, sems,
):
    def coil_copy(coil, part):
        return pltpu.make_async_copy(
            coils_hbm.at[part, coil], coils_ref.at[part, coil], coil_sems.at[part, coil]
        )

    def coil_group(group):
        coils = [coil for pair in GROUPS[group] for coil in pair if coil >= EARLY]
        return [coil_copy(coil, part) for coil in coils for part in range(2)]

    for group in range(2):
        for copy in coil_group(group):
            copy.start()
    orders = [
        pltpu.make_async_copy(source, target, sems.at[i])
        for i, (source, target) in enumerate(
            [(depth_hbm, depth_ref), (panel_hbm, panel_ref)]
        )
    ]
    for copy in orders:
        copy.start()
    for d in range(GROUP):
        here = slice(d * PART, (d + 1) * PART)
        words = images_ref[d]
        scale = scale_up(words[36:37].astype(F32))
        for part, values in enumerate(pair_apart(words[0:36])):
            values = values * scale
            for block in range(3):
                field_ref[part, here, block * 128 : (block + 1) * 128] = values[
                    block * PART : (block + 1) * PART
                ]
    lines_ref[:, 0 : 2 * N] = ahead_ref[...]
    lines_ref[0:96, 2 * N : 4 * N] = ahead_ref[0:96, :]
    lines_ref[96:192, 2 * N : 4 * N] = jnp.zeros((96, 2 * N), BF16)
    rows_ref[:, 0:96] = adjoint_ref[:, 0:96]
    rows_ref[:, 96:192] = adjoint_ref[:, 0:96]
    rows_ref[:, 192:288] = adjoint_ref[:, 96:192]

    def coil_maps(coil):
        source = early_ref if coil < EARLY else coils_ref
        return (
            jnp.concatenate([source[part, coil, 0], source[part, coil, 1]], 1).astype(F32)
            for part in range(2)
        )

    def terms_of(coil):
        coil_re, coil_im = coil_maps(coil)
        field_re, field_im = field_ref[0], field_ref[1]
        re_high, re_low = split(coil_re * field_re - coil_im * field_im)
        im_high, im_low = split(coil_re * field_im + coil_im * field_re)
        return jnp.concatenate([re_high, im_high, re_low, im_low], 0)

    def side(values, i):
        return values[:, i * 2 * N : (i + 1) * 2 * N]

    def go_ahead(coils):
        first = dot(lines_ref[...], jnp.concatenate([terms_of(coil) for coil in coils], 1))
        for i, coil in enumerate(coils):
            here = side(first, i)
            high, low = split(here[0:96] + here[96:192] - back_ref[coil])
            resid_ref[coil, 0:96] = high
            resid_ref[coil, 96:192] = low
            resid_ref[coil, 192:288] = high

    def go_back(coils):
        both = dot(rows_ref[...], jnp.concatenate([resid_ref[coil] for coil in coils], 1))
        total_re = total_im = 0.0
        for i, coil in enumerate(coils):
            coil_re, coil_im = coil_maps(coil)
            rows_re, rows_im = side(both, i)[0:N], side(both, i)[N : 2 * N]
            total_re += coil_re * rows_re + coil_im * rows_im
            total_im += coil_re * rows_im - coil_im * rows_re
        return total_re, total_im

    for group, pairs in enumerate(GROUPS):
        for copy in coil_group(group):
            copy.wait()
        if group + 2 < len(GROUPS):
            for copy in coil_group(group + 2):
                copy.start()
        for coils in pairs:
            go_ahead(coils)
    for group, pairs in enumerate(GROUPS):
        for i, coils in enumerate(pairs):
            grad_re, grad_im = go_back(coils)
            if group == i == 0:
                grad_ref[0], grad_ref[1] = grad_re, grad_im
            else:
                grad_ref[0] += grad_re
                grad_ref[1] += grad_im
    for copy in orders:
        copy.wait()
    parts = []
    for part in range(2):
        for pos in range(2):
            high, low = split(grad_ref[part, :, pos * N : (pos + 1) * N])
            moved = dot(depth_ref[...], high, (1, 1)) + dot(depth_ref[...], low, (1, 1))
            parts.append(moved.reshape(PART, GROUP, N))
    largest = functools.reduce(jnp.maximum, map(jnp.abs, parts))
    largest = jnp.max(largest, axis=0)
    for shift in (1, 2, 4, 4):
        ahead = jnp.concatenate([largest[:, shift:], largest[:, :shift]], 1)
        largest = jnp.maximum(largest, ahead)
    high, low = split(level_of(largest))
    level = dot(high, panel_ref[...]) + dot(low, panel_ref[...])
    scale = scale_down(level)[None]
    words = [pair_up(parts[pos] * scale, parts[2 + pos] * scale) for pos in range(2)]
    level = level.astype(jnp.int32)
    for d in range(GROUP):
        lanes = slice(d * PART, (d + 1) * PART)
        pieces = [words[pos][zz, :, lanes] for zz in range(PART) for pos in range(2)]
        pieces.append(jnp.broadcast_to(level[:, d * PART : d * PART + 1], (GROUP, WIDE - VOX)))
        out_ref[d * GROUP : (d + 1) * GROUP, 0, :] = jnp.concatenate(pieces, 1)


def model(images, back, early, ahead, adjoint, coils, depth_order, panel):
    return pl.pallas_call(
        model_kernel,
        out_shape=jax.ShapeDtypeStruct((GROUP * GROUP, 1, WIDE), jnp.int32),
        in_specs=[VMEM] * 5 + [HBM] * 3,
        out_specs=VMEM,
        scratch_shapes=[
            pltpu.VMEM((2, COILS, 2, N, N), BF16),
            pltpu.VMEM((N, N), BF16),
            pltpu.VMEM((N, N), BF16),
            pltpu.VMEM((2, N, 2 * N), F32),
            pltpu.VMEM((2, N, 2 * N), F32),
            pltpu.VMEM((4 * LINES, 4 * N), BF16),
            pltpu.VMEM((2 * N, 6 * LINES), BF16),
            pltpu.VMEM((COILS, 6 * LINES, 2 * N), BF16),
            DMA((2, COILS)),
            DMA((2,)),
        ],
        compiler_params=pltpu.CompilerParams(vmem_limit_bytes=32 * MIB),
        name="model",
    )(
        images,
        *map(in_vmem, (back, early, ahead, adjoint)),
        *map(in_hbm, (coils, depth_order, panel)),
    )


def update_kernel(grads_ref, weights_ref, pick_ref, slab_ref, out_ref):
    words = grads_ref[:, 0, :].T
    scale = scale_up(words[VOX : VOX + 1].astype(F32))
    real, imag = pair_apart(words[0:VOX])
    high, low = split(jnp.concatenate([real * scale, imag * scale], 1))
    grad = dot(high, weights_ref[...]) + dot(low, weights_ref[...])
    high, low = split(grad)
    grad = dot(pick_ref[...], high) + dot(pick_ref[...], low)
    out_ref[0] = slab_ref[0] - STEP_SIZE * grad[:, 0:RANK]
    out_ref[1] = slab_ref[1] - STEP_SIZE * grad[:, RANK : 2 * RANK]


def update(grads, weights, pick, slab):
    return pl.pallas_call(
        update_kernel,
        out_shape=jax.ShapeDtypeStruct((2, 2 * PART * PART, RANK), F32),
        in_specs=[VMEM] * 4,
        out_specs=VMEM,
        compiler_params=pltpu.CompilerParams(vmem_limit_bytes=16 * MIB),
        name="update",
    )(grads, weights, pick, slab)


def on_device(spatial_basis, temporal, coil_maps, kspace_data, sampled_lines):
    table = {name: jnp.asarray(value) for name, value in constants().items()}
    flat_temporal = temporal.reshape(2 * RANK, GROUP * GROUP)
    flat_basis = jnp.transpose(spatial_basis, (0, 1, 3, 2, 4)).reshape(2 * RANK, PART, 2, N)
    sent = frames(flat_basis, flat_temporal, table["spread"], table["inside"])
    images = lax.all_to_all(sent, "dev", 0, 0, tiled=True)
    back, early, ahead, adjoint, weights = data_back(
        kspace_data, coil_maps, sampled_lines, table["dft"], flat_temporal, table["frame_order"]
    )
    sent = model(
        images, back, early, ahead, adjoint, coil_maps, table["depth_order"], table["panel"]
    )
    grads = lax.all_to_all(sent, ("dev", "grp"), 0, 0, tiled=True)
    slab = lax.dynamic_slice_in_dim(spatial_basis, lax.axis_index("grp") * PART, PART, 4)
    slab = jnp.transpose(slab, (0, 3, 4, 2, 1)).reshape(2, 2 * PART * PART, RANK).astype(F32)
    result = update(grads, weights, table["pick"], slab)
    return jnp.transpose(result.reshape(2, PART, PART, 2, RANK), (0, 4, 3, 1, 2))


def solution(mesh):
    placed = (
        P(None, None, None, "dev", None),
        P(),
        P(),
        P(("grp", "dev"), None, None, None, None, None),
        P(("grp", "dev"), None),
    )
    return jax.shard_map(
        on_device,
        mesh=mesh,
        in_specs=placed,
        out_specs=P(None, None, None, "dev", "grp"),
        check_vma=False,
    )
```

```python
import functools
import math

import jax
import jax.numpy as jnp
import numpy as np
from jax import lax
from jax.experimental import pallas as pl
from jax.experimental.pallas import tpu as pltpu
from jax.sharding import PartitionSpec as P

STEP_SIZE = 0.25
N = 192
PART = 12
ROWS = 4
RANK = 32
COILS = 16
LINES = 48
EARLY = 1
GROUPS = [[(0,)], [(1, 2)], [(3, 4), (5, 6)], [(7, 8), (9, 10)], [(11, 12), (13, 14), (15,)]]
CHUNK = 4
GROUP = 16
VOX = 2 * PART * PART
SLOT = 16
LANES = 128
WIDE = 384
STEPS = 8.0
TOP = 15.0
F32 = jnp.float32
BF16 = jnp.bfloat16
VMEM = pl.BlockSpec(memory_space=pltpu.VMEM)
HBM = pl.BlockSpec(memory_space=pltpu.HBM)
in_hbm = lambda array: pltpu.with_memory_space_constraint(array, pltpu.HBM)
in_vmem = lambda array: pltpu.with_memory_space_constraint(array, pltpu.VMEM)
DMA = pltpu.SemaphoreType.DMA
MIB = 1024 * 1024


def swap_slots(pieces):
    slot = lax.broadcasted_iota(jnp.int32, pieces[0].shape, 1) // SLOT
    pieces = list(pieces)
    for step in (1, 2, 4):
        lower = jnp.bitwise_and(slot, step) == 0
        for i in range(len(pieces)):
            if i & step == 0:
                first, second = pieces[i], pieces[i + step]
                pieces[i] = jnp.where(lower, first, pltpu.roll(second, step * SLOT, 1))
                pieces[i + step] = jnp.where(
                    lower, pltpu.roll(first, LANES - step * SLOT, 1), second
                )
    return pieces


def largest_of_slot(values):
    lane = lax.broadcasted_iota(jnp.int32, values.shape, 1)
    for step in (1, 2, 4, 8):
        partner = jnp.where(
            jnp.bitwise_and(lane, step) == 0,
            pltpu.roll(values, LANES - step, 1),
            pltpu.roll(values, step, 1),
        )
        values = jnp.maximum(values, partner)
    return values


def level_of(largest):
    return jnp.ceil(jnp.log2(jnp.maximum(largest, 1e-30)) * STEPS)


def scale_down(level):
    return jnp.exp2(TOP - level / STEPS)


def scale_up(level):
    return jnp.exp2(level / STEPS - TOP)


def pair_up(real, imag):
    real, imag = (
        jnp.clip(jnp.floor(part + 0.5), -32768.0, 32767.0).astype(jnp.int32)
        for part in (real, imag)
    )
    return jnp.bitwise_or(jnp.left_shift(real, 16), jnp.bitwise_and(imag, 65535))


def pair_apart(words):
    real = jnp.right_shift(words, 16)
    imag = jnp.right_shift(jnp.left_shift(words, 16), 16)
    return real.astype(F32), imag.astype(F32)


def two_terms(values):
    high = values.astype(np.float32).astype(jnp.bfloat16)
    low = (values - high.astype(np.float64)).astype(jnp.bfloat16)
    return high, low


def split(values):
    high = values.astype(BF16)
    return high, (values - high.astype(F32)).astype(BF16)


def dot(left, right, over=(1, 0)):
    return lax.dot_general(
        left, right, (((over[0],), (over[1],)), ((), ())), preferred_element_type=F32
    )


def constants():
    places = np.arange(N)
    angles = (places[:, None] * places[None, :] % N) * (2.0 * math.pi / N)
    cos_pair = two_terms(np.cos(angles) / math.sqrt(N))
    sin_pair = two_terms(np.sin(angles) / math.sqrt(N))
    dft = np.stack([*cos_pair, *sin_pair])
    columns = np.arange(2 * RANK * 2 * ROWS)
    spread = columns[None, :] // (2 * ROWS) == np.arange(2 * RANK)[:, None]
    rows = np.arange(2 * ROWS)
    inside = columns[None, :] % (2 * ROWS) == ((rows % ROWS) * 2 + rows // ROWS)[:, None]
    order = np.arange(N)
    depth_order = ((order % GROUP) * PART + order // GROUP)[:, None] == places[None, :]
    peers = np.arange(GROUP * GROUP)
    frame_order = ((peers % GROUP) * GROUP + peers // GROUP)[:, None] == peers[None, :]
    out = np.arange(VOX)
    row, zz, pos = out // (2 * PART), out // 2 % PART, out % 2
    pick = ((zz * 2 + pos) * SLOT + row)[:, None] == np.arange(WIDE)[None, :]
    return dict(
        dft=dft,
        spread=spread.astype(jnp.bfloat16),
        inside=inside.astype(np.float32),
        depth_order=depth_order.astype(jnp.bfloat16),
        frame_order=frame_order.astype(jnp.bfloat16),
        pick=pick.astype(jnp.bfloat16),
    )


def frames_kernel(
    basis_hbm, temporal_hbm, spread_hbm, inside_hbm, out_ref,
    basis_ref, temporal_ref, spread_ref, inside_ref, mix_ref, basis_sem, sems,
):
    copies = [
        pltpu.make_async_copy(source, target, sems.at[i])
        for i, (source, target) in enumerate(
            [
                (temporal_hbm, temporal_ref),
                (spread_hbm, spread_ref),
                (inside_hbm, inside_ref),
            ]
        )
    ]
    whole = pltpu.make_async_copy(basis_hbm, basis_ref, basis_sem)
    whole.start()
    for copy in copies:
        copy.start()
    copies[0].wait()
    first = lax.axis_index("grp") * GROUP
    frame = lax.broadcasted_iota(jnp.int32, (GROUP, GROUP * GROUP), 0) + first
    column = lax.broadcasted_iota(jnp.int32, (GROUP, GROUP * GROUP), 1)
    chosen = (frame == column).astype(F32).astype(BF16)
    weights = dot(chosen, temporal_ref[...], (1, 1))
    lane = lax.broadcasted_iota(jnp.int32, (GROUP, 2 * RANK), 1)
    from_lane = lax.broadcasted_iota(jnp.int32, (2 * RANK, 2 * RANK), 0)
    to_lane = lax.broadcasted_iota(jnp.int32, (2 * RANK, 2 * RANK), 1)
    apart = jnp.abs(from_lane - to_lane) == RANK
    swapped = dot(weights.astype(BF16), apart.astype(F32).astype(BF16))
    copies[1].wait()
    signed = jnp.where(lane < RANK, weights, -weights)
    wide_re = dot(signed.astype(BF16), spread_ref[...])
    wide_im = dot(swapped.astype(BF16), spread_ref[...])
    copies[2].wait()
    inside = inside_ref[...]
    wide = jnp.concatenate([wide_re[:, None], wide_im[:, None]], 1)
    mix = inside[None, None] * wide[:, :, None]
    mix_ref[...] = mix.reshape(2 * GROUP * 2 * ROWS, wide_re.shape[1]).astype(BF16)
    images = []
    whole.wait()
    for i in range(PART // ROWS):
        basis = basis_ref[:, i * ROWS : (i + 1) * ROWS].reshape(2 * RANK * 2 * ROWS, N)
        images.append(dot(mix_ref[...], basis).reshape(GROUP, 2, 2 * ROWS, N))
    largest = functools.reduce(jnp.maximum, [jnp.max(jnp.abs(image), axis=1) for image in images])
    largest = jnp.max(jnp.max(largest, axis=1, keepdims=True), axis=2, keepdims=True)
    level = level_of(largest)
    scale = scale_down(level)
    for i, image in enumerate(images):
        words = pair_up(image[:, 0] * scale, image[:, 1] * scale)
        words = jnp.concatenate([words[:, 0:ROWS], words[:, ROWS : 2 * ROWS]], 2)
        for block in range(3):
            at = block * PART + i * ROWS
            out_ref[:, at : at + ROWS, :] = words[:, :, block * 128 : (block + 1) * 128]
    out_ref[:, 36:40, :] = jnp.broadcast_to(level, (GROUP, 4, 128)).astype(jnp.int32)


def frames(basis, temporal, spread, inside):
    rows = 2 * RANK * 2 * ROWS
    return pl.pallas_call(
        frames_kernel,
        out_shape=jax.ShapeDtypeStruct((GROUP, 40, 128), jnp.int32),
        in_specs=[HBM] * 4,
        out_specs=VMEM,
        scratch_shapes=[
            pltpu.VMEM((2 * RANK, PART, 2, N), BF16),
            pltpu.VMEM((2 * RANK, GROUP * GROUP), BF16),
            pltpu.VMEM((2 * RANK, rows), BF16),
            pltpu.VMEM((2 * ROWS, rows), F32),
            pltpu.VMEM((2 * GROUP * 2 * ROWS, rows), BF16),
            DMA(()),
            DMA((3,)),
        ],
        compiler_params=pltpu.CompilerParams(vmem_limit_bytes=16 * MIB),
        name="frames",
    )(*map(in_hbm, (basis, temporal, spread, inside)))


def data_kernel(
    data_hbm, coils_hbm, lines_hbm, dft_hbm, temporal_hbm, order_hbm,
    back_ref, early_ref, ahead_ref, adjoint_ref, weights_ref,
    data_ref, lines_ref, dft_ref, temporal_ref, order_ref, data_sems, sems,
):
    small = [
        pltpu.make_async_copy(source, target, sems.at[i])
        for i, (source, target) in enumerate(
            [
                (dft_hbm, dft_ref),
                (lines_hbm, lines_ref),
                (temporal_hbm, temporal_ref),
                (order_hbm, order_ref),
                (coils_hbm.at[:, pl.ds(0, EARLY)], early_ref),
            ]
        )
    ]
    chunks = [
        pltpu.make_async_copy(
            data_hbm.at[0, :, pl.ds(i * CHUNK, CHUNK)],
            data_ref.at[:, pl.ds(i * CHUNK, CHUNK)],
            data_sems.at[i],
        )
        for i in range(COILS // CHUNK)
    ]
    small[0].start()
    small[1].start()
    chunks[0].start()
    for copy in small[2:] + chunks[1:]:
        copy.start()
    small[0].wait()
    small[1].wait()
    places = lax.broadcasted_iota(jnp.int32, (N, LINES), 0)
    chosen = (places == lines_ref[...]).astype(F32)
    chosen_rows = chosen.T.astype(BF16)
    chosen = chosen.astype(BF16)
    for term in range(2):
        cos_line = dot(chosen_rows, dft_ref[term])
        sin_line = dot(chosen_rows, dft_ref[2 + term])
        from_re = jnp.concatenate([cos_line, -sin_line], 0).astype(BF16)
        from_im = jnp.concatenate([sin_line, cos_line], 0).astype(BF16)
        at = term * 96
        ahead_ref[at : at + 96, 0:N] = jnp.concatenate([cos_line, -sin_line], 0).astype(BF16)
        ahead_ref[at : at + 96, N : 2 * N] = jnp.concatenate([sin_line, cos_line], 0).astype(BF16)
        cos_back = dot(dft_ref[term], chosen)
        sin_back = dot(dft_ref[2 + term], chosen)
        adjoint_ref[0:N, at : at + 48] = cos_back.astype(BF16)
        adjoint_ref[0:N, at + 48 : at + 96] = (-sin_back).astype(BF16)
        adjoint_ref[N : 2 * N, at : at + 48] = sin_back.astype(BF16)
        adjoint_ref[N : 2 * N, at + 48 : at + 96] = cos_back.astype(BF16)

    def through(high, low, which):
        return (
            dot(high, dft_ref[which])
            + dot(low, dft_ref[which])
            + dot(high, dft_ref[which + 1])
        )

    for i in range(COILS // CHUNK):
        chunks[i].wait()
        here = slice(i * CHUNK, (i + 1) * CHUNK)
        re_high, re_low = split(data_ref[0, here].reshape(CHUNK * 2 * LINES, N))
        im_high, im_low = split(data_ref[1, here].reshape(CHUNK * 2 * LINES, N))
        back_re = through(re_high, re_low, 0) - through(im_high, im_low, 2)
        back_im = through(re_high, re_low, 2) + through(im_high, im_low, 0)
        for part, values in enumerate((back_re, back_im)):
            values = values.reshape(CHUNK, 2, LINES, N)
            at = slice(part * LINES, (part + 1) * LINES)
            for pos in range(2):
                back_ref[here, at, pos * N : (pos + 1) * N] = values[:, pos]
    small[2].wait()
    small[3].wait()
    small[4].wait()
    weights = dot(order_ref[...], temporal_ref[...], (1, 1)).astype(BF16)
    peers = GROUP * GROUP
    weights_ref[0:peers, 0:RANK] = weights[:, 0:RANK]
    weights_ref[0:peers, RANK : 2 * RANK] = -weights[:, RANK : 2 * RANK]
    weights_ref[peers : 2 * peers, 0:RANK] = weights[:, RANK : 2 * RANK]
    weights_ref[peers : 2 * peers, RANK : 2 * RANK] = weights[:, 0:RANK]


def data_back(data, coils, lines, dft, temporal, order):
    return pl.pallas_call(
        data_kernel,
        out_shape=(
            pltpu.VMEM((COILS, 2 * LINES, 2 * N), F32),
            pltpu.VMEM((2, EARLY, 2, N, N), BF16),
            pltpu.VMEM((4 * LINES, 2 * N), BF16),
            pltpu.VMEM((2 * N, 4 * LINES), BF16),
            jax.ShapeDtypeStruct((2 * GROUP * GROUP, 2 * RANK), BF16),
        ),
        in_specs=[HBM] * 6,
        out_specs=(VMEM,) * 5,
        scratch_shapes=[
            pltpu.VMEM((2, COILS, 2, LINES, N), F32),
            pltpu.VMEM((1, LINES), jnp.int32),
            pltpu.VMEM((4, N, N), BF16),
            pltpu.VMEM((2 * RANK, GROUP * GROUP), BF16),
            pltpu.VMEM((GROUP * GROUP, GROUP * GROUP), BF16),
            DMA((COILS // CHUNK,)),
            DMA((5,)),
        ],
        compiler_params=pltpu.CompilerParams(vmem_limit_bytes=16 * MIB),
        name="data_back",
    )(*map(in_hbm, (data, coils, lines, dft, temporal, order)))


def model_kernel(
    images_ref, back_ref, early_ref, ahead_ref, adjoint_ref, coils_hbm, depth_hbm,
    out_ref, coils_ref, depth_ref, padded_ref, field_ref, grad_ref,
    lines_ref, rows_ref, resid_ref, coil_sems, sem,
):
    def coil_copy(coil, part):
        return pltpu.make_async_copy(
            coils_hbm.at[part, coil], coils_ref.at[part, coil], coil_sems.at[part, coil]
        )

    def coil_group(group):
        coils = [coil for pair in GROUPS[group] for coil in pair if coil >= EARLY]
        return [coil_copy(coil, part) for coil in coils for part in range(2)]

    for group in range(2):
        for copy in coil_group(group):
            copy.start()
    order = pltpu.make_async_copy(depth_hbm, depth_ref, sem)
    order.start()
    for d in range(GROUP):
        here = slice(d * PART, (d + 1) * PART)
        words = images_ref[d]
        scale = scale_up(words[36:37].astype(F32))
        for part, values in enumerate(pair_apart(words[0:36])):
            values = values * scale
            for block in range(3):
                field_ref[part, here, block * 128 : (block + 1) * 128] = values[
                    block * PART : (block + 1) * PART
                ]
    lines_ref[:, 0 : 2 * N] = ahead_ref[...]
    lines_ref[0:96, 2 * N : 4 * N] = ahead_ref[0:96, :]
    lines_ref[96:192, 2 * N : 4 * N] = jnp.zeros((96, 2 * N), BF16)
    rows_ref[:, 0:96] = adjoint_ref[:, 0:96]
    rows_ref[:, 96:192] = adjoint_ref[:, 0:96]
    rows_ref[:, 192:288] = adjoint_ref[:, 96:192]

    def coil_maps(coil):
        source = early_ref if coil < EARLY else coils_ref
        return (
            jnp.concatenate([source[part, coil, 0], source[part, coil, 1]], 1).astype(F32)
            for part in range(2)
        )

    def terms_of(coil):
        coil_re, coil_im = coil_maps(coil)
        field_re, field_im = field_ref[0], field_ref[1]
        re_high, re_low = split(coil_re * field_re - coil_im * field_im)
        im_high, im_low = split(coil_re * field_im + coil_im * field_re)
        return jnp.concatenate([re_high, im_high, re_low, im_low], 0)

    def side(values, i):
        return values[:, i * 2 * N : (i + 1) * 2 * N]

    def go_ahead(coils):
        first = dot(lines_ref[...], jnp.concatenate([terms_of(coil) for coil in coils], 1))
        for i, coil in enumerate(coils):
            here = side(first, i)
            high, low = split(here[0:96] + here[96:192] - back_ref[coil])
            resid_ref[coil, 0:96] = high
            resid_ref[coil, 96:192] = low
            resid_ref[coil, 192:288] = high

    def go_back(coils):
        both = dot(rows_ref[...], jnp.concatenate([resid_ref[coil] for coil in coils], 1))
        total_re = total_im = 0.0
        for i, coil in enumerate(coils):
            coil_re, coil_im = coil_maps(coil)
            rows_re, rows_im = side(both, i)[0:N], side(both, i)[N : 2 * N]
            total_re += coil_re * rows_re + coil_im * rows_im
            total_im += coil_re * rows_im - coil_im * rows_re
        return total_re, total_im

    for group, pairs in enumerate(GROUPS):
        for copy in coil_group(group):
            copy.wait()
        if group + 2 < len(GROUPS):
            for copy in coil_group(group + 2):
                copy.start()
        for coils in pairs:
            go_ahead(coils)
    for group, pairs in enumerate(GROUPS):
        for i, coils in enumerate(pairs):
            grad_re, grad_im = go_back(coils)
            if group == i == 0:
                grad_ref[0], grad_ref[1] = grad_re, grad_im
            else:
                grad_ref[0] += grad_re
                grad_ref[1] += grad_im
    order.wait()
    for d in range(GROUP):
        at = d * SLOT
        padded_ref[:, at : at + PART] = grad_ref[:, d * PART : (d + 1) * PART]
        padded_ref[:, at + PART : at + SLOT] = jnp.zeros((2, SLOT - PART, 2 * N), F32)
    parts = []
    for part in range(2):
        for pos in range(2):
            high, low = split(padded_ref[part, :, pos * N : (pos + 1) * N])
            moved = dot(depth_ref[...], high, (1, 1)) + dot(depth_ref[...], low, (1, 1))
            parts.append(moved.reshape(PART, GROUP, GROUP * SLOT))
    largest = jnp.max(functools.reduce(jnp.maximum, map(jnp.abs, parts)), axis=0)
    lane = lax.broadcasted_iota(jnp.int32, (GROUP, LANES), 1)
    for half in range(2):
        lanes = slice(half * LANES, (half + 1) * LANES)
        level = level_of(largest_of_slot(largest[:, lanes]))
        scale = scale_down(level)
        level = level.astype(jnp.int32)
        words = [
            jnp.where(
                jnp.bitwise_and(lane, SLOT - 1) < PART,
                pair_up(parts[pos][zz, :, lanes] * scale, parts[2 + pos][zz, :, lanes] * scale),
                level,
            )
            for zz in range(PART)
            for pos in range(2)
        ]
        for block in range(WIDE // LANES):
            swapped = swap_slots(words[block * 8 : (block + 1) * 8])
            for i, values in enumerate(swapped):
                at = (half * 8 + i) * GROUP
                out_ref[at : at + GROUP, 0, block * LANES : (block + 1) * LANES] = values


def model(images, back, early, ahead, adjoint, coils, depth_order):
    return pl.pallas_call(
        model_kernel,
        out_shape=jax.ShapeDtypeStruct((GROUP * GROUP, 1, WIDE), jnp.int32),
        in_specs=[VMEM] * 5 + [HBM] * 2,
        out_specs=VMEM,
        scratch_shapes=[
            pltpu.VMEM((2, COILS, 2, N, N), BF16),
            pltpu.VMEM((N, N), BF16),
            pltpu.VMEM((2, GROUP * SLOT, 2 * N), F32),
            pltpu.VMEM((2, N, 2 * N), F32),
            pltpu.VMEM((2, N, 2 * N), F32),
            pltpu.VMEM((4 * LINES, 4 * N), BF16),
            pltpu.VMEM((2 * N, 6 * LINES), BF16),
            pltpu.VMEM((COILS, 6 * LINES, 2 * N), BF16),
            DMA((2, COILS)),
            DMA(()),
        ],
        compiler_params=pltpu.CompilerParams(vmem_limit_bytes=32 * MIB),
        name="model",
    )(
        images,
        *map(in_vmem, (back, early, ahead, adjoint)),
        *map(in_hbm, (coils, depth_order)),
    )


def update_kernel(grads_ref, weights_ref, pick_ref, slab_ref, out_ref):
    words = grads_ref[:, 0, :].T
    scale = scale_up(words[PART : PART + 1].astype(F32))
    real, imag = pair_apart(words)
    high, low = split(jnp.concatenate([real * scale, imag * scale], 1))
    grad = dot(high, weights_ref[...]) + dot(low, weights_ref[...])
    high, low = split(grad)
    grad = dot(pick_ref[...], high) + dot(pick_ref[...], low)
    out_ref[0] = slab_ref[0] - STEP_SIZE * grad[:, 0:RANK]
    out_ref[1] = slab_ref[1] - STEP_SIZE * grad[:, RANK : 2 * RANK]


def update(grads, weights, pick, slab):
    return pl.pallas_call(
        update_kernel,
        out_shape=jax.ShapeDtypeStruct((2, 2 * PART * PART, RANK), F32),
        in_specs=[VMEM] * 4,
        out_specs=VMEM,
        compiler_params=pltpu.CompilerParams(vmem_limit_bytes=16 * MIB),
        name="update",
    )(grads, weights, pick, slab)


def on_device(spatial_basis, temporal, coil_maps, kspace_data, sampled_lines):
    table = {name: jnp.asarray(value) for name, value in constants().items()}
    flat_temporal = temporal.reshape(2 * RANK, GROUP * GROUP)
    flat_basis = jnp.transpose(spatial_basis, (0, 1, 3, 2, 4)).reshape(2 * RANK, PART, 2, N)
    sent = frames(flat_basis, flat_temporal, table["spread"], table["inside"])
    images = lax.all_to_all(sent, "dev", 0, 0, tiled=True)
    back, early, ahead, adjoint, weights = data_back(
        kspace_data, coil_maps, sampled_lines, table["dft"], flat_temporal, table["frame_order"]
    )
    sent = model(
        images, back, early, ahead, adjoint, coil_maps, table["depth_order"]
    )
    grads = lax.all_to_all(sent, ("dev", "grp"), 0, 0, tiled=True)
    slab = lax.dynamic_slice_in_dim(spatial_basis, lax.axis_index("grp") * PART, PART, 4)
    slab = jnp.transpose(slab, (0, 3, 4, 2, 1)).reshape(2, 2 * PART * PART, RANK).astype(F32)
    result = update(grads, weights, table["pick"], slab)
    return jnp.transpose(result.reshape(2, PART, PART, 2, RANK), (0, 4, 3, 1, 2))


def solution(mesh):
    placed = (
        P(None, None, None, "dev", None),
        P(),
        P(),
        P(("grp", "dev"), None, None, None, None, None),
        P(("grp", "dev"), None),
    )
    return jax.shard_map(
        on_device,
        mesh=mesh,
        in_specs=placed,
        out_specs=P(None, None, None, "dev", "grp"),
        check_vma=False,
    )
```

```python
import functools
import math

import jax
import jax.numpy as jnp
import numpy as np
from jax import lax
from jax.experimental import pallas as pl
from jax.experimental.pallas import tpu as pltpu
from jax.sharding import PartitionSpec as P

STEP_SIZE = 0.25
N = 192
PART = 12
ROWS = 4
RANK = 32
COILS = 16
LINES = 48
EARLY = 1
GROUPS = [[(0,)], [(1, 2)], [(3, 4), (5, 6)], [(7, 8), (9, 10)], [(11, 12), (13, 14), (15,)]]
CHUNK = 16
GROUP = 16
VOX = 2 * PART * PART
SLOT = 16
LANES = 128
WIDE = 384
STEPS = 8.0
TOP = 15.0
F32 = jnp.float32
BF16 = jnp.bfloat16
VMEM = pl.BlockSpec(memory_space=pltpu.VMEM)
HBM = pl.BlockSpec(memory_space=pltpu.HBM)
in_hbm = lambda array: pltpu.with_memory_space_constraint(array, pltpu.HBM)
in_vmem = lambda array: pltpu.with_memory_space_constraint(array, pltpu.VMEM)
DMA = pltpu.SemaphoreType.DMA
MIB = 1024 * 1024


def swap_slots(pieces):
    slot = lax.broadcasted_iota(jnp.int32, pieces[0].shape, 1) // SLOT
    pieces = list(pieces)
    for step in (1, 2, 4):
        lower = jnp.bitwise_and(slot, step) == 0
        for i in range(len(pieces)):
            if i & step == 0:
                first, second = pieces[i], pieces[i + step]
                pieces[i] = jnp.where(lower, first, pltpu.roll(second, step * SLOT, 1))
                pieces[i + step] = jnp.where(
                    lower, pltpu.roll(first, LANES - step * SLOT, 1), second
                )
    return pieces


def largest_of_slot(values):
    lane = lax.broadcasted_iota(jnp.int32, values.shape, 1)
    for step in (1, 2, 4, 8):
        partner = jnp.where(
            jnp.bitwise_and(lane, step) == 0,
            pltpu.roll(values, LANES - step, 1),
            pltpu.roll(values, step, 1),
        )
        values = jnp.maximum(values, partner)
    return values


def level_of(largest):
    return jnp.ceil(jnp.log2(jnp.maximum(largest, 1e-30)) * STEPS)


def scale_down(level):
    return jnp.exp2(TOP - level / STEPS)


def scale_up(level):
    return jnp.exp2(level / STEPS - TOP)


def pair_up(real, imag):
    real, imag = (
        jnp.clip(jnp.floor(part + 0.5), -32768.0, 32767.0).astype(jnp.int32)
        for part in (real, imag)
    )
    return jnp.bitwise_or(jnp.left_shift(real, 16), jnp.bitwise_and(imag, 65535))


def pair_apart(words):
    real = jnp.right_shift(words, 16)
    imag = jnp.right_shift(jnp.left_shift(words, 16), 16)
    return real.astype(F32), imag.astype(F32)


def two_terms(values):
    high = values.astype(np.float32).astype(jnp.bfloat16)
    low = (values - high.astype(np.float64)).astype(jnp.bfloat16)
    return high, low


def split(values):
    high = values.astype(BF16)
    return high, (values - high.astype(F32)).astype(BF16)


def dot(left, right, over=(1, 0)):
    return lax.dot_general(
        left, right, (((over[0],), (over[1],)), ((), ())), preferred_element_type=F32
    )


def constants():
    places = np.arange(N)
    angles = (places[:, None] * places[None, :] % N) * (2.0 * math.pi / N)
    cos_pair = two_terms(np.cos(angles) / math.sqrt(N))
    sin_pair = two_terms(np.sin(angles) / math.sqrt(N))
    sum_pair = two_terms((np.cos(angles) + np.sin(angles)) / math.sqrt(N))
    dft = np.stack([*cos_pair, *sin_pair, *sum_pair])
    columns = np.arange(2 * RANK * 2 * ROWS)
    spread = columns[None, :] // (2 * ROWS) == np.arange(2 * RANK)[:, None]
    rows = np.arange(2 * ROWS)
    inside = columns[None, :] % (2 * ROWS) == ((rows % ROWS) * 2 + rows // ROWS)[:, None]
    order = np.arange(N)
    depth_order = ((order % GROUP) * PART + order // GROUP)[:, None] == places[None, :]
    peers = np.arange(GROUP * GROUP)
    frame_order = ((peers % GROUP) * GROUP + peers // GROUP)[:, None] == peers[None, :]
    out = np.arange(VOX)
    row, zz, pos = out // (2 * PART), out // 2 % PART, out % 2
    pick = ((zz * 2 + pos) * SLOT + row)[:, None] == np.arange(WIDE)[None, :]
    return dict(
        dft=dft,
        spread=spread.astype(jnp.bfloat16),
        inside=inside.astype(np.float32),
        depth_order=depth_order.astype(jnp.bfloat16),
        frame_order=frame_order.astype(jnp.bfloat16),
        pick=pick.astype(jnp.bfloat16),
    )


def frames_kernel(
    basis_hbm, temporal_hbm, spread_hbm, inside_hbm, out_ref,
    basis_ref, temporal_ref, spread_ref, inside_ref, mix_ref, basis_sem, sems,
):
    copies = [
        pltpu.make_async_copy(source, target, sems.at[i])
        for i, (source, target) in enumerate(
            [
                (temporal_hbm, temporal_ref),
                (spread_hbm, spread_ref),
                (inside_hbm, inside_ref),
            ]
        )
    ]
    whole = pltpu.make_async_copy(basis_hbm, basis_ref, basis_sem)
    whole.start()
    for copy in copies:
        copy.start()
    copies[0].wait()
    first = lax.axis_index("grp") * GROUP
    frame = lax.broadcasted_iota(jnp.int32, (GROUP, GROUP * GROUP), 0) + first
    column = lax.broadcasted_iota(jnp.int32, (GROUP, GROUP * GROUP), 1)
    chosen = (frame == column).astype(F32).astype(BF16)
    weights = dot(chosen, temporal_ref[...], (1, 1))
    lane = lax.broadcasted_iota(jnp.int32, (GROUP, 2 * RANK), 1)
    from_lane = lax.broadcasted_iota(jnp.int32, (2 * RANK, 2 * RANK), 0)
    to_lane = lax.broadcasted_iota(jnp.int32, (2 * RANK, 2 * RANK), 1)
    apart = jnp.abs(from_lane - to_lane) == RANK
    swapped = dot(weights.astype(BF16), apart.astype(F32).astype(BF16))
    copies[1].wait()
    signed = jnp.where(lane < RANK, weights, -weights)
    wide_re = dot(signed.astype(BF16), spread_ref[...])
    wide_im = dot(swapped.astype(BF16), spread_ref[...])
    copies[2].wait()
    inside = inside_ref[...]
    wide = jnp.concatenate([wide_re[:, None], wide_im[:, None]], 1)
    mix = inside[None, None] * wide[:, :, None]
    mix_ref[...] = mix.reshape(2 * GROUP * 2 * ROWS, wide_re.shape[1]).astype(BF16)
    images = []
    whole.wait()
    for i in range(PART // ROWS):
        basis = basis_ref[:, i * ROWS : (i + 1) * ROWS].reshape(2 * RANK * 2 * ROWS, N)
        images.append(dot(mix_ref[...], basis).reshape(GROUP, 2, 2 * ROWS, N))
    largest = functools.reduce(jnp.maximum, [jnp.max(jnp.abs(image), axis=1) for image in images])
    largest = jnp.max(jnp.max(largest, axis=1, keepdims=True), axis=2, keepdims=True)
    level = level_of(largest)
    scale = scale_down(level)
    for i, image in enumerate(images):
        words = pair_up(image[:, 0] * scale, image[:, 1] * scale)
        words = jnp.concatenate([words[:, 0:ROWS], words[:, ROWS : 2 * ROWS]], 2)
        for block in range(3):
            at = block * PART + i * ROWS
            out_ref[:, at : at + ROWS, :] = words[:, :, block * 128 : (block + 1) * 128]
    out_ref[:, 36:40, :] = jnp.broadcast_to(level, (GROUP, 4, 128)).astype(jnp.int32)


def frames(basis, temporal, spread, inside):
    rows = 2 * RANK * 2 * ROWS
    return pl.pallas_call(
        frames_kernel,
        out_shape=jax.ShapeDtypeStruct((GROUP, 40, 128), jnp.int32),
        in_specs=[HBM] * 4,
        out_specs=VMEM,
        scratch_shapes=[
            pltpu.VMEM((2 * RANK, PART, 2, N), BF16),
            pltpu.VMEM((2 * RANK, GROUP * GROUP), BF16),
            pltpu.VMEM((2 * RANK, rows), BF16),
            pltpu.VMEM((2 * ROWS, rows), F32),
            pltpu.VMEM((2 * GROUP * 2 * ROWS, rows), BF16),
            DMA(()),
            DMA((3,)),
        ],
        compiler_params=pltpu.CompilerParams(vmem_limit_bytes=16 * MIB),
        name="frames",
    )(*map(in_hbm, (basis, temporal, spread, inside)))


def data_kernel(
    data_hbm, coils_hbm, lines_hbm, dft_hbm, temporal_hbm, order_hbm,
    back_ref, early_ref, ahead_ref, adjoint_ref, weights_ref,
    data_ref, lines_ref, dft_ref, temporal_ref, order_ref, data_sems, sems,
):
    small = [
        pltpu.make_async_copy(source, target, sems.at[i])
        for i, (source, target) in enumerate(
            [
                (dft_hbm, dft_ref),
                (lines_hbm, lines_ref),
                (temporal_hbm, temporal_ref),
                (order_hbm, order_ref),
                (coils_hbm.at[:, pl.ds(0, EARLY)], early_ref),
            ]
        )
    ]
    chunks = [
        pltpu.make_async_copy(
            data_hbm.at[0, :, pl.ds(i * CHUNK, CHUNK)],
            data_ref.at[:, pl.ds(i * CHUNK, CHUNK)],
            data_sems.at[i],
        )
        for i in range(COILS // CHUNK)
    ]
    small[0].start()
    small[1].start()
    chunks[0].start()
    for copy in small[2:] + chunks[1:]:
        copy.start()
    small[0].wait()
    small[1].wait()
    places = lax.broadcasted_iota(jnp.int32, (N, LINES), 0)
    chosen = (places == lines_ref[...]).astype(F32)
    chosen_rows = chosen.T.astype(BF16)
    chosen = chosen.astype(BF16)
    for term in range(2):
        cos_line = dot(chosen_rows, dft_ref[term])
        sin_line = dot(chosen_rows, dft_ref[2 + term])
        from_re = jnp.concatenate([cos_line, -sin_line], 0).astype(BF16)
        from_im = jnp.concatenate([sin_line, cos_line], 0).astype(BF16)
        at = term * 96
        ahead_ref[at : at + 96, 0:N] = jnp.concatenate([cos_line, -sin_line], 0).astype(BF16)
        ahead_ref[at : at + 96, N : 2 * N] = jnp.concatenate([sin_line, cos_line], 0).astype(BF16)
        cos_back = dot(dft_ref[term], chosen)
        sin_back = dot(dft_ref[2 + term], chosen)
        adjoint_ref[0:N, at : at + 48] = cos_back.astype(BF16)
        adjoint_ref[0:N, at + 48 : at + 96] = (-sin_back).astype(BF16)
        adjoint_ref[N : 2 * N, at : at + 48] = sin_back.astype(BF16)
        adjoint_ref[N : 2 * N, at + 48 : at + 96] = cos_back.astype(BF16)

    def through(values, which):
        high, low = split(values)
        return (
            dot(high, dft_ref[which])
            + dot(low, dft_ref[which])
            + dot(high, dft_ref[which + 1])
        )

    for i in range(COILS // CHUNK):
        chunks[i].wait()
        here = slice(i * CHUNK, (i + 1) * CHUNK)
        data_re = data_ref[0, here].reshape(CHUNK * 2 * LINES, N)
        data_im = data_ref[1, here].reshape(CHUNK * 2 * LINES, N)
        by_cos, by_sin = through(data_re, 0), through(data_im, 2)
        back_re = by_cos - by_sin
        back_im = through(data_re + data_im, 4) - by_cos - by_sin
        for part, values in enumerate((back_re, back_im)):
            values = values.reshape(CHUNK, 2, LINES, N)
            at = slice(part * LINES, (part + 1) * LINES)
            for pos in range(2):
                back_ref[here, at, pos * N : (pos + 1) * N] = values[:, pos]
    small[2].wait()
    small[3].wait()
    small[4].wait()
    weights = dot(order_ref[...], temporal_ref[...], (1, 1)).astype(BF16)
    peers = GROUP * GROUP
    weights_ref[0:peers, 0:RANK] = weights[:, 0:RANK]
    weights_ref[0:peers, RANK : 2 * RANK] = -weights[:, RANK : 2 * RANK]
    weights_ref[peers : 2 * peers, 0:RANK] = weights[:, RANK : 2 * RANK]
    weights_ref[peers : 2 * peers, RANK : 2 * RANK] = weights[:, 0:RANK]


def data_back(data, coils, lines, dft, temporal, order):
    return pl.pallas_call(
        data_kernel,
        out_shape=(
            pltpu.VMEM((COILS, 2 * LINES, 2 * N), F32),
            pltpu.VMEM((2, EARLY, 2, N, N), BF16),
            pltpu.VMEM((4 * LINES, 2 * N), BF16),
            pltpu.VMEM((2 * N, 4 * LINES), BF16),
            jax.ShapeDtypeStruct((2 * GROUP * GROUP, 2 * RANK), BF16),
        ),
        in_specs=[HBM] * 6,
        out_specs=(VMEM,) * 5,
        scratch_shapes=[
            pltpu.VMEM((2, COILS, 2, LINES, N), F32),
            pltpu.VMEM((1, LINES), jnp.int32),
            pltpu.VMEM((6, N, N), BF16),
            pltpu.VMEM((2 * RANK, GROUP * GROUP), BF16),
            pltpu.VMEM((GROUP * GROUP, GROUP * GROUP), BF16),
            DMA((COILS // CHUNK,)),
            DMA((5,)),
        ],
        compiler_params=pltpu.CompilerParams(vmem_limit_bytes=16 * MIB),
        name="data_back",
    )(*map(in_hbm, (data, coils, lines, dft, temporal, order)))


def model_kernel(
    images_ref, back_ref, early_ref, ahead_ref, adjoint_ref, coils_hbm, depth_hbm,
    out_ref, coils_ref, depth_ref, padded_ref, field_ref, grad_ref,
    lines_ref, rows_ref, resid_ref, coil_sems, sem,
):
    def coil_copy(coil, part):
        return pltpu.make_async_copy(
            coils_hbm.at[part, coil], coils_ref.at[part, coil], coil_sems.at[part, coil]
        )

    def coil_group(group):
        coils = [coil for pair in GROUPS[group] for coil in pair if coil >= EARLY]
        return [coil_copy(coil, part) for coil in coils for part in range(2)]

    for group in range(2):
        for copy in coil_group(group):
            copy.start()
    order = pltpu.make_async_copy(depth_hbm, depth_ref, sem)
    order.start()
    for d in range(GROUP):
        here = slice(d * PART, (d + 1) * PART)
        words = images_ref[d]
        scale = scale_up(words[36:37].astype(F32))
        for part, values in enumerate(pair_apart(words[0:36])):
            values = values * scale
            for block in range(3):
                field_ref[part, here, block * 128 : (block + 1) * 128] = values[
                    block * PART : (block + 1) * PART
                ]
    lines_ref[:, 0 : 2 * N] = ahead_ref[...]
    lines_ref[0:96, 2 * N : 4 * N] = ahead_ref[0:96, :]
    lines_ref[96:192, 2 * N : 4 * N] = jnp.zeros((96, 2 * N), BF16)
    rows_ref[:, 0:96] = adjoint_ref[:, 0:96]
    rows_ref[:, 96:192] = adjoint_ref[:, 0:96]
    rows_ref[:, 192:288] = adjoint_ref[:, 96:192]

    def coil_maps(coil):
        source = early_ref if coil < EARLY else coils_ref
        return (
            jnp.concatenate([source[part, coil, 0], source[part, coil, 1]], 1).astype(F32)
            for part in range(2)
        )

    def terms_of(coil):
        coil_re, coil_im = coil_maps(coil)
        field_re, field_im = field_ref[0], field_ref[1]
        re_high, re_low = split(coil_re * field_re - coil_im * field_im)
        im_high, im_low = split(coil_re * field_im + coil_im * field_re)
        return jnp.concatenate([re_high, im_high, re_low, im_low], 0)

    def side(values, i):
        return values[:, i * 2 * N : (i + 1) * 2 * N]

    def go_ahead(coils):
        first = dot(lines_ref[...], jnp.concatenate([terms_of(coil) for coil in coils], 1))
        for i, coil in enumerate(coils):
            here = side(first, i)
            high, low = split(here[0:96] + here[96:192] - back_ref[coil])
            resid_ref[coil, 0:96] = high
            resid_ref[coil, 96:192] = low
            resid_ref[coil, 192:288] = high

    def go_back(coils):
        both = dot(rows_ref[...], jnp.concatenate([resid_ref[coil] for coil in coils], 1))
        total_re = total_im = 0.0
        for i, coil in enumerate(coils):
            coil_re, coil_im = coil_maps(coil)
            rows_re, rows_im = side(both, i)[0:N], side(both, i)[N : 2 * N]
            total_re += coil_re * rows_re + coil_im * rows_im
            total_im += coil_re * rows_im - coil_im * rows_re
        return total_re, total_im

    for group, pairs in enumerate(GROUPS):
        for copy in coil_group(group):
            copy.wait()
        if group + 2 < len(GROUPS):
            for copy in coil_group(group + 2):
                copy.start()
        for coils in pairs:
            go_ahead(coils)
    for group, pairs in enumerate(GROUPS):
        for i, coils in enumerate(pairs):
            grad_re, grad_im = go_back(coils)
            if group == i == 0:
                grad_ref[0], grad_ref[1] = grad_re, grad_im
            else:
                grad_ref[0] += grad_re
                grad_ref[1] += grad_im
    order.wait()
    for d in range(GROUP):
        at = d * SLOT
        padded_ref[:, at : at + PART] = grad_ref[:, d * PART : (d + 1) * PART]
        padded_ref[:, at + PART : at + SLOT] = jnp.zeros((2, SLOT - PART, 2 * N), F32)
    parts = []
    for part in range(2):
        for pos in range(2):
            high, low = split(padded_ref[part, :, pos * N : (pos + 1) * N])
            moved = dot(depth_ref[...], high, (1, 1)) + dot(depth_ref[...], low, (1, 1))
            parts.append(moved.reshape(PART, GROUP, GROUP * SLOT))
    largest = jnp.max(functools.reduce(jnp.maximum, map(jnp.abs, parts)), axis=0)
    lane = lax.broadcasted_iota(jnp.int32, (GROUP, LANES), 1)
    for half in range(2):
        lanes = slice(half * LANES, (half + 1) * LANES)
        level = level_of(largest_of_slot(largest[:, lanes]))
        scale = scale_down(level)
        level = level.astype(jnp.int32)
        words = [
            jnp.where(
                jnp.bitwise_and(lane, SLOT - 1) < PART,
                pair_up(parts[pos][zz, :, lanes] * scale, parts[2 + pos][zz, :, lanes] * scale),
                level,
            )
            for zz in range(PART)
            for pos in range(2)
        ]
        for block in range(WIDE // LANES):
            swapped = swap_slots(words[block * 8 : (block + 1) * 8])
            for i, values in enumerate(swapped):
                at = (half * 8 + i) * GROUP
                out_ref[at : at + GROUP, 0, block * LANES : (block + 1) * LANES] = values


def model(images, back, early, ahead, adjoint, coils, depth_order):
    return pl.pallas_call(
        model_kernel,
        out_shape=jax.ShapeDtypeStruct((GROUP * GROUP, 1, WIDE), jnp.int32),
        in_specs=[VMEM] * 5 + [HBM] * 2,
        out_specs=VMEM,
        scratch_shapes=[
            pltpu.VMEM((2, COILS, 2, N, N), BF16),
            pltpu.VMEM((N, N), BF16),
            pltpu.VMEM((2, GROUP * SLOT, 2 * N), F32),
            pltpu.VMEM((2, N, 2 * N), F32),
            pltpu.VMEM((2, N, 2 * N), F32),
            pltpu.VMEM((4 * LINES, 4 * N), BF16),
            pltpu.VMEM((2 * N, 6 * LINES), BF16),
            pltpu.VMEM((COILS, 6 * LINES, 2 * N), BF16),
            DMA((2, COILS)),
            DMA(()),
        ],
        compiler_params=pltpu.CompilerParams(vmem_limit_bytes=32 * MIB),
        name="model",
    )(
        images,
        *map(in_vmem, (back, early, ahead, adjoint)),
        *map(in_hbm, (coils, depth_order)),
    )


def update_kernel(grads_ref, weights_ref, pick_ref, slab_ref, out_ref):
    words = grads_ref[:, 0, :].T
    scale = scale_up(words[PART : PART + 1].astype(F32))
    real, imag = pair_apart(words)
    high, low = split(jnp.concatenate([real * scale, imag * scale], 1))
    grad = dot(high, weights_ref[...]) + dot(low, weights_ref[...])
    high, low = split(grad)
    grad = dot(pick_ref[...], high) + dot(pick_ref[...], low)
    out_ref[0] = slab_ref[0] - STEP_SIZE * grad[:, 0:RANK]
    out_ref[1] = slab_ref[1] - STEP_SIZE * grad[:, RANK : 2 * RANK]


def update(grads, weights, pick, slab):
    return pl.pallas_call(
        update_kernel,
        out_shape=jax.ShapeDtypeStruct((2, 2 * PART * PART, RANK), F32),
        in_specs=[VMEM] * 4,
        out_specs=VMEM,
        compiler_params=pltpu.CompilerParams(vmem_limit_bytes=16 * MIB),
        name="update",
    )(grads, weights, pick, slab)


def on_device(spatial_basis, temporal, coil_maps, kspace_data, sampled_lines):
    table = {name: jnp.asarray(value) for name, value in constants().items()}
    flat_temporal = temporal.reshape(2 * RANK, GROUP * GROUP)
    flat_basis = jnp.transpose(spatial_basis, (0, 1, 3, 2, 4)).reshape(2 * RANK, PART, 2, N)
    sent = frames(flat_basis, flat_temporal, table["spread"], table["inside"])
    images = lax.all_to_all(sent, "dev", 0, 0, tiled=True)
    back, early, ahead, adjoint, weights = data_back(
        kspace_data, coil_maps, sampled_lines, table["dft"], flat_temporal, table["frame_order"]
    )
    sent = model(
        images, back, early, ahead, adjoint, coil_maps, table["depth_order"]
    )
    grads = lax.all_to_all(sent, ("dev", "grp"), 0, 0, tiled=True)
    slab = lax.dynamic_slice_in_dim(spatial_basis, lax.axis_index("grp") * PART, PART, 4)
    slab = jnp.transpose(slab, (0, 3, 4, 2, 1)).reshape(2, 2 * PART * PART, RANK).astype(F32)
    result = update(grads, weights, table["pick"], slab)
    return jnp.transpose(result.reshape(2, PART, PART, 2, RANK), (0, 4, 3, 1, 2))


def solution(mesh):
    placed = (
        P(None, None, None, "dev", None),
        P(),
        P(),
        P(("grp", "dev"), None, None, None, None, None),
        P(("grp", "dev"), None),
    )
    return jax.shard_map(
        on_device,
        mesh=mesh,
        in_specs=placed,
        out_specs=P(None, None, None, "dev", "grp"),
        check_vma=False,
    )
```

```python
import functools
import math

import jax
import jax.numpy as jnp
import numpy as np
from jax import lax
from jax.experimental import pallas as pl
from jax.experimental.pallas import tpu as pltpu
from jax.sharding import PartitionSpec as P

STEP_SIZE = 0.25
N = 192
PART = 12
ROWS = 4
RANK = 32
COILS = 16
LINES = 48
EARLY = 1
GROUPS = [[(0,)], [(1, 2)], [(3, 4), (5, 6)], [(7, 8), (9, 10)], [(11, 12), (13, 14), (15,)]]
CHUNK = 16
GROUP = 16
VOX = 2 * PART * PART
SLOT = 16
LANES = 128
WIDE = 384
STEPS = 8.0
TOP = 15.0
F32 = jnp.float32
BF16 = jnp.bfloat16
VMEM = pl.BlockSpec(memory_space=pltpu.VMEM)
HBM = pl.BlockSpec(memory_space=pltpu.HBM)
in_hbm = lambda array: pltpu.with_memory_space_constraint(array, pltpu.HBM)
in_vmem = lambda array: pltpu.with_memory_space_constraint(array, pltpu.VMEM)
DMA = pltpu.SemaphoreType.DMA
MIB = 1024 * 1024


def swap_slots(pieces):
    slot = lax.broadcasted_iota(jnp.int32, pieces[0].shape, 1) // SLOT
    pieces = list(pieces)
    for step in (1, 2, 4):
        lower = jnp.bitwise_and(slot, step) == 0
        for i in range(len(pieces)):
            if i & step == 0:
                first, second = pieces[i], pieces[i + step]
                pieces[i] = jnp.where(lower, first, pltpu.roll(second, step * SLOT, 1))
                pieces[i + step] = jnp.where(
                    lower, pltpu.roll(first, LANES - step * SLOT, 1), second
                )
    return pieces


def largest_of_slot(values):
    lane = lax.broadcasted_iota(jnp.int32, values.shape, 1)
    for step in (1, 2, 4, 8):
        partner = jnp.where(
            jnp.bitwise_and(lane, step) == 0,
            pltpu.roll(values, LANES - step, 1),
            pltpu.roll(values, step, 1),
        )
        values = jnp.maximum(values, partner)
    return values


def level_of(largest):
    return jnp.ceil(jnp.log2(jnp.maximum(largest, 1e-30)) * STEPS)


def scale_down(level):
    return jnp.exp2(TOP - level / STEPS)


def scale_up(level):
    return jnp.exp2(level / STEPS - TOP)


def pair_up(real, imag):
    real, imag = (
        jnp.clip(jnp.floor(part + 0.5), -32768.0, 32767.0).astype(jnp.int32)
        for part in (real, imag)
    )
    return jnp.bitwise_or(jnp.left_shift(real, 16), jnp.bitwise_and(imag, 65535))


def pair_apart(words):
    real = jnp.right_shift(words, 16)
    imag = jnp.right_shift(jnp.left_shift(words, 16), 16)
    return real.astype(F32), imag.astype(F32)


def two_terms(values):
    high = values.astype(np.float32).astype(jnp.bfloat16)
    low = (values - high.astype(np.float64)).astype(jnp.bfloat16)
    return high, low


def split(values):
    high = values.astype(BF16)
    return high, (values - high.astype(F32)).astype(BF16)


def dot(left, right, over=(1, 0)):
    return lax.dot_general(
        left, right, (((over[0],), (over[1],)), ((), ())), preferred_element_type=F32
    )


def constants():
    places = np.arange(N)
    angles = (places[:, None] * places[None, :] % N) * (2.0 * math.pi / N)
    cos_pair = two_terms(np.cos(angles) / math.sqrt(N))
    sin_pair = two_terms(np.sin(angles) / math.sqrt(N))
    sum_pair = two_terms((np.cos(angles) + np.sin(angles)) / math.sqrt(N))
    dft = np.stack([*cos_pair, *sin_pair, *sum_pair])
    columns = np.arange(2 * RANK * 2 * ROWS)
    spread = columns[None, :] // (2 * ROWS) == np.arange(2 * RANK)[:, None]
    rows = np.arange(2 * ROWS)
    inside = columns[None, :] % (2 * ROWS) == ((rows % ROWS) * 2 + rows // ROWS)[:, None]
    order = np.arange(N)
    depth_order = ((order % GROUP) * PART + order // GROUP)[:, None] == places[None, :]
    peers = np.arange(GROUP * GROUP)
    frame_order = ((peers % GROUP) * GROUP + peers // GROUP)[:, None] == peers[None, :]
    out = np.arange(VOX)
    row, zz, pos = out // (2 * PART), out // 2 % PART, out % 2
    pick = ((zz * 2 + pos) * SLOT + row)[:, None] == np.arange(WIDE)[None, :]
    return dict(
        dft=dft,
        spread=spread.astype(jnp.bfloat16),
        inside=inside.astype(np.float32),
        depth_order=depth_order.astype(jnp.bfloat16),
        frame_order=frame_order.astype(jnp.bfloat16),
        pick=pick.astype(jnp.bfloat16),
    )


def frames_kernel(
    basis_hbm, temporal_hbm, spread_hbm, inside_hbm, out_ref,
    basis_ref, temporal_ref, spread_ref, inside_ref, mix_ref, basis_sem, sems,
):
    copies = [
        pltpu.make_async_copy(source, target, sems.at[i])
        for i, (source, target) in enumerate(
            [
                (temporal_hbm, temporal_ref),
                (spread_hbm, spread_ref),
                (inside_hbm, inside_ref),
            ]
        )
    ]
    whole = pltpu.make_async_copy(basis_hbm, basis_ref, basis_sem)
    whole.start()
    for copy in copies:
        copy.start()
    copies[0].wait()
    first = lax.axis_index("grp") * GROUP
    frame = lax.broadcasted_iota(jnp.int32, (GROUP, GROUP * GROUP), 0) + first
    column = lax.broadcasted_iota(jnp.int32, (GROUP, GROUP * GROUP), 1)
    chosen = (frame == column).astype(F32).astype(BF16)
    weights = dot(chosen, temporal_ref[...], (1, 1))
    lane = lax.broadcasted_iota(jnp.int32, (GROUP, 2 * RANK), 1)
    from_lane = lax.broadcasted_iota(jnp.int32, (2 * RANK, 2 * RANK), 0)
    to_lane = lax.broadcasted_iota(jnp.int32, (2 * RANK, 2 * RANK), 1)
    apart = jnp.abs(from_lane - to_lane) == RANK
    swapped = dot(weights.astype(BF16), apart.astype(F32).astype(BF16))
    copies[1].wait()
    signed = jnp.where(lane < RANK, weights, -weights)
    wide_re = dot(signed.astype(BF16), spread_ref[...])
    wide_im = dot(swapped.astype(BF16), spread_ref[...])
    copies[2].wait()
    inside = inside_ref[...]
    wide = jnp.concatenate([wide_re[:, None], wide_im[:, None]], 1)
    mix = inside[None, None] * wide[:, :, None]
    mix_ref[...] = mix.reshape(2 * GROUP * 2 * ROWS, wide_re.shape[1]).astype(BF16)
    images = []
    whole.wait()
    for i in range(PART // ROWS):
        basis = basis_ref[:, i * ROWS : (i + 1) * ROWS].reshape(2 * RANK * 2 * ROWS, N)
        images.append(dot(mix_ref[...], basis).reshape(GROUP, 2, 2 * ROWS, N))
    largest = functools.reduce(jnp.maximum, [jnp.max(jnp.abs(image), axis=1) for image in images])
    largest = jnp.max(jnp.max(largest, axis=1, keepdims=True), axis=2, keepdims=True)
    level = level_of(largest)
    scale = scale_down(level)
    for i, image in enumerate(images):
        words = pair_up(image[:, 0] * scale, image[:, 1] * scale)
        words = jnp.concatenate([words[:, 0:ROWS], words[:, ROWS : 2 * ROWS]], 2)
        for block in range(3):
            at = block * PART + i * ROWS
            out_ref[:, at : at + ROWS, :] = words[:, :, block * 128 : (block + 1) * 128]
    out_ref[:, 36:40, :] = jnp.broadcast_to(level, (GROUP, 4, 128)).astype(jnp.int32)


def frames(basis, temporal, spread, inside):
    rows = 2 * RANK * 2 * ROWS
    return pl.pallas_call(
        frames_kernel,
        out_shape=jax.ShapeDtypeStruct((GROUP, 40, 128), jnp.int32),
        in_specs=[HBM] * 4,
        out_specs=VMEM,
        scratch_shapes=[
            pltpu.VMEM((2 * RANK, PART, 2, N), BF16),
            pltpu.VMEM((2 * RANK, GROUP * GROUP), BF16),
            pltpu.VMEM((2 * RANK, rows), BF16),
            pltpu.VMEM((2 * ROWS, rows), F32),
            pltpu.VMEM((2 * GROUP * 2 * ROWS, rows), BF16),
            DMA(()),
            DMA((3,)),
        ],
        compiler_params=pltpu.CompilerParams(vmem_limit_bytes=16 * MIB),
        name="frames",
    )(*map(in_hbm, (basis, temporal, spread, inside)))


def data_kernel(
    data_hbm, coils_hbm, lines_hbm, dft_hbm, temporal_hbm, order_hbm,
    back_ref, early_ref, ahead_ref, adjoint_ref, weights_ref,
    data_ref, lines_ref, dft_ref, temporal_ref, order_ref, data_sems, sems,
):
    small = [
        pltpu.make_async_copy(source, target, sems.at[i])
        for i, (source, target) in enumerate(
            [
                (dft_hbm, dft_ref),
                (lines_hbm, lines_ref),
                (temporal_hbm, temporal_ref),
                (order_hbm, order_ref),
                (coils_hbm.at[:, pl.ds(0, EARLY)], early_ref),
            ]
        )
    ]
    chunks = [
        pltpu.make_async_copy(
            data_hbm.at[0, :, pl.ds(i * CHUNK, CHUNK)],
            data_ref.at[:, pl.ds(i * CHUNK, CHUNK)],
            data_sems.at[i],
        )
        for i in range(COILS // CHUNK)
    ]
    small[0].start()
    small[1].start()
    chunks[0].start()
    for copy in small[2:] + chunks[1:]:
        copy.start()
    small[0].wait()
    small[1].wait()
    places = lax.broadcasted_iota(jnp.int32, (N, LINES), 0)
    chosen = (places == lines_ref[...]).astype(F32)
    chosen_rows = chosen.T.astype(BF16)
    chosen = chosen.astype(BF16)
    for term in range(2):
        cos_line = dot(chosen_rows, dft_ref[term])
        sin_line = dot(chosen_rows, dft_ref[2 + term])
        from_re = jnp.concatenate([cos_line, -sin_line], 0).astype(BF16)
        from_im = jnp.concatenate([sin_line, cos_line], 0).astype(BF16)
        at = term * 96
        ahead_ref[at : at + 96, 0:N] = jnp.concatenate([cos_line, -sin_line], 0).astype(BF16)
        ahead_ref[at : at + 96, N : 2 * N] = jnp.concatenate([sin_line, cos_line], 0).astype(BF16)
        cos_back = dot(dft_ref[term], chosen)
        sin_back = dot(dft_ref[2 + term], chosen)
        adjoint_ref[0:N, at : at + 48] = cos_back.astype(BF16)
        adjoint_ref[0:N, at + 48 : at + 96] = (-sin_back).astype(BF16)
        adjoint_ref[N : 2 * N, at : at + 48] = sin_back.astype(BF16)
        adjoint_ref[N : 2 * N, at + 48 : at + 96] = cos_back.astype(BF16)

    def through(values, which):
        high, low = split(values)
        return (
            dot(high, dft_ref[which])
            + dot(low, dft_ref[which])
            + dot(high, dft_ref[which + 1])
        )

    for i in range(COILS // CHUNK):
        chunks[i].wait()
        here = slice(i * CHUNK, (i + 1) * CHUNK)
        data_re = data_ref[0, here].reshape(CHUNK * 2 * LINES, N)
        data_im = data_ref[1, here].reshape(CHUNK * 2 * LINES, N)
        by_cos, by_sin = through(data_re, 0), through(data_im, 2)
        back_re = by_cos - by_sin
        back_im = through(data_re + data_im, 4) - by_cos - by_sin
        for part, values in enumerate((back_re, back_im)):
            values = values.reshape(CHUNK, 2, LINES, N)
            at = slice(part * LINES, (part + 1) * LINES)
            for pos in range(2):
                back_ref[here, at, pos * N : (pos + 1) * N] = values[:, pos]
    small[2].wait()
    small[3].wait()
    small[4].wait()
    weights = dot(order_ref[...], temporal_ref[...], (1, 1)).astype(BF16)
    peers = GROUP * GROUP
    weights_ref[0:peers, 0:RANK] = weights[:, 0:RANK]
    weights_ref[0:peers, RANK : 2 * RANK] = -weights[:, RANK : 2 * RANK]
    weights_ref[peers : 2 * peers, 0:RANK] = weights[:, RANK : 2 * RANK]
    weights_ref[peers : 2 * peers, RANK : 2 * RANK] = weights[:, 0:RANK]


def data_back(data, coils, lines, dft, temporal, order):
    return pl.pallas_call(
        data_kernel,
        out_shape=(
            pltpu.VMEM((COILS, 2 * LINES, 2 * N), F32),
            pltpu.VMEM((2, EARLY, 2, N, N), BF16),
            pltpu.VMEM((4 * LINES, 2 * N), BF16),
            pltpu.VMEM((2 * N, 4 * LINES), BF16),
            jax.ShapeDtypeStruct((2 * GROUP * GROUP, 2 * RANK), BF16),
        ),
        in_specs=[HBM] * 6,
        out_specs=(VMEM,) * 5,
        scratch_shapes=[
            pltpu.VMEM((2, COILS, 2, LINES, N), F32),
            pltpu.VMEM((1, LINES), jnp.int32),
            pltpu.VMEM((6, N, N), BF16),
            pltpu.VMEM((2 * RANK, GROUP * GROUP), BF16),
            pltpu.VMEM((GROUP * GROUP, GROUP * GROUP), BF16),
            DMA((COILS // CHUNK,)),
            DMA((5,)),
        ],
        compiler_params=pltpu.CompilerParams(vmem_limit_bytes=16 * MIB),
        name="data_back",
    )(*map(in_hbm, (data, coils, lines, dft, temporal, order)))


def model_kernel(
    images_ref, back_ref, early_ref, ahead_ref, adjoint_ref, coils_hbm, depth_hbm,
    out_ref, coils_ref, depth_ref, padded_ref, field_ref, grad_ref,
    lines_ref, rows_ref, resid_ref, coil_sems, sem,
):
    def coil_copy(coil, part):
        return pltpu.make_async_copy(
            coils_hbm.at[part, coil], coils_ref.at[part, coil], coil_sems.at[part, coil]
        )

    def coil_group(group):
        coils = [coil for pair in GROUPS[group] for coil in pair if coil >= EARLY]
        return [coil_copy(coil, part) for coil in coils for part in range(2)]

    for group in range(2):
        for copy in coil_group(group):
            copy.start()
    order = pltpu.make_async_copy(depth_hbm, depth_ref, sem)
    order.start()
    for d in range(GROUP):
        here = slice(d * PART, (d + 1) * PART)
        words = images_ref[d]
        scale = scale_up(words[36:37].astype(F32))
        for part, values in enumerate(pair_apart(words[0:36])):
            values = values * scale
            for block in range(3):
                field_ref[part, here, block * 128 : (block + 1) * 128] = values[
                    block * PART : (block + 1) * PART
                ]
    lines_ref[:, 0 : 2 * N] = ahead_ref[...]
    lines_ref[0:96, 2 * N : 4 * N] = ahead_ref[0:96, :]
    lines_ref[96:192, 2 * N : 4 * N] = jnp.zeros((96, 2 * N), BF16)
    rows_ref[:, 0:96] = adjoint_ref[:, 0:96]
    rows_ref[:, 96:192] = adjoint_ref[:, 0:96]
    rows_ref[:, 192:288] = adjoint_ref[:, 96:192]

    def coil_maps(coil):
        source = early_ref if coil < EARLY else coils_ref
        return (
            jnp.concatenate([source[part, coil, 0], source[part, coil, 1]], 1).astype(F32)
            for part in range(2)
        )

    def terms_of(coil):
        coil_re, coil_im = coil_maps(coil)
        field_re, field_im = field_ref[0], field_ref[1]
        re_high, re_low = split(coil_re * field_re - coil_im * field_im)
        im_high, im_low = split(coil_re * field_im + coil_im * field_re)
        return jnp.concatenate([re_high, im_high, re_low, im_low], 0)

    def side(values, i):
        return values[:, i * 2 * N : (i + 1) * 2 * N]

    def go_ahead(coils):
        first = dot(lines_ref[...], jnp.concatenate([terms_of(coil) for coil in coils], 1))
        for i, coil in enumerate(coils):
            here = side(first, i)
            high, low = split(here[0:96] + here[96:192] - back_ref[coil])
            resid_ref[coil, 0:96] = high
            resid_ref[coil, 96:192] = low
            resid_ref[coil, 192:288] = high

    def go_back(coils):
        both = dot(rows_ref[...], jnp.concatenate([resid_ref[coil] for coil in coils], 1))
        total_re = total_im = 0.0
        for i, coil in enumerate(coils):
            coil_re, coil_im = coil_maps(coil)
            rows_re, rows_im = side(both, i)[0:N], side(both, i)[N : 2 * N]
            total_re += coil_re * rows_re + coil_im * rows_im
            total_im += coil_re * rows_im - coil_im * rows_re
        return total_re, total_im

    for group, pairs in enumerate(GROUPS):
        for copy in coil_group(group):
            copy.wait()
        if group + 2 < len(GROUPS):
            for copy in coil_group(group + 2):
                copy.start()
        for coils in pairs:
            go_ahead(coils)
    for first in range(0, COILS, 4):
        grad_re, grad_im = go_back(range(first, first + 4))
        if first == 0:
            grad_ref[0], grad_ref[1] = grad_re, grad_im
        else:
            grad_ref[0] += grad_re
            grad_ref[1] += grad_im
    order.wait()
    for d in range(GROUP):
        at = d * SLOT
        padded_ref[:, at : at + PART] = grad_ref[:, d * PART : (d + 1) * PART]
        padded_ref[:, at + PART : at + SLOT] = jnp.zeros((2, SLOT - PART, 2 * N), F32)
    parts = []
    for part in range(2):
        for pos in range(2):
            high, low = split(padded_ref[part, :, pos * N : (pos + 1) * N])
            moved = dot(depth_ref[...], high, (1, 1)) + dot(depth_ref[...], low, (1, 1))
            parts.append(moved.reshape(PART, GROUP, GROUP * SLOT))
    largest = jnp.max(functools.reduce(jnp.maximum, map(jnp.abs, parts)), axis=0)
    lane = lax.broadcasted_iota(jnp.int32, (GROUP, LANES), 1)
    for half in range(2):
        lanes = slice(half * LANES, (half + 1) * LANES)
        level = level_of(largest_of_slot(largest[:, lanes]))
        scale = scale_down(level)
        level = level.astype(jnp.int32)
        words = [
            jnp.where(
                jnp.bitwise_and(lane, SLOT - 1) < PART,
                pair_up(parts[pos][zz, :, lanes] * scale, parts[2 + pos][zz, :, lanes] * scale),
                level,
            )
            for zz in range(PART)
            for pos in range(2)
        ]
        for block in range(WIDE // LANES):
            swapped = swap_slots(words[block * 8 : (block + 1) * 8])
            for i, values in enumerate(swapped):
                at = (half * 8 + i) * GROUP
                out_ref[at : at + GROUP, 0, block * LANES : (block + 1) * LANES] = values


def model(images, back, early, ahead, adjoint, coils, depth_order):
    return pl.pallas_call(
        model_kernel,
        out_shape=jax.ShapeDtypeStruct((GROUP * GROUP, 1, WIDE), jnp.int32),
        in_specs=[VMEM] * 5 + [HBM] * 2,
        out_specs=VMEM,
        scratch_shapes=[
            pltpu.VMEM((2, COILS, 2, N, N), BF16),
            pltpu.VMEM((N, N), BF16),
            pltpu.VMEM((2, GROUP * SLOT, 2 * N), F32),
            pltpu.VMEM((2, N, 2 * N), F32),
            pltpu.VMEM((2, N, 2 * N), F32),
            pltpu.VMEM((4 * LINES, 4 * N), BF16),
            pltpu.VMEM((2 * N, 6 * LINES), BF16),
            pltpu.VMEM((COILS, 6 * LINES, 2 * N), BF16),
            DMA((2, COILS)),
            DMA(()),
        ],
        compiler_params=pltpu.CompilerParams(vmem_limit_bytes=32 * MIB),
        name="model",
    )(
        images,
        *map(in_vmem, (back, early, ahead, adjoint)),
        *map(in_hbm, (coils, depth_order)),
    )


def update_kernel(grads_ref, weights_ref, pick_ref, slab_ref, out_ref):
    words = grads_ref[:, 0, :].T
    scale = scale_up(words[PART : PART + 1].astype(F32))
    real, imag = pair_apart(words)
    high, low = split(jnp.concatenate([real * scale, imag * scale], 1))
    grad = dot(high, weights_ref[...]) + dot(low, weights_ref[...])
    high, low = split(grad)
    grad = dot(pick_ref[...], high) + dot(pick_ref[...], low)
    out_ref[0] = slab_ref[0] - STEP_SIZE * grad[:, 0:RANK]
    out_ref[1] = slab_ref[1] - STEP_SIZE * grad[:, RANK : 2 * RANK]


def update(grads, weights, pick, slab):
    return pl.pallas_call(
        update_kernel,
        out_shape=jax.ShapeDtypeStruct((2, 2 * PART * PART, RANK), F32),
        in_specs=[VMEM] * 4,
        out_specs=VMEM,
        compiler_params=pltpu.CompilerParams(vmem_limit_bytes=16 * MIB),
        name="update",
    )(grads, weights, pick, slab)


def on_device(spatial_basis, temporal, coil_maps, kspace_data, sampled_lines):
    table = {name: jnp.asarray(value) for name, value in constants().items()}
    flat_temporal = temporal.reshape(2 * RANK, GROUP * GROUP)
    flat_basis = jnp.transpose(spatial_basis, (0, 1, 3, 2, 4)).reshape(2 * RANK, PART, 2, N)
    sent = frames(flat_basis, flat_temporal, table["spread"], table["inside"])
    images = lax.all_to_all(sent, "dev", 0, 0, tiled=True)
    back, early, ahead, adjoint, weights = data_back(
        kspace_data, coil_maps, sampled_lines, table["dft"], flat_temporal, table["frame_order"]
    )
    sent = model(
        images, back, early, ahead, adjoint, coil_maps, table["depth_order"]
    )
    grads = lax.all_to_all(sent, ("dev", "grp"), 0, 0, tiled=True)
    slab = lax.dynamic_slice_in_dim(spatial_basis, lax.axis_index("grp") * PART, PART, 4)
    slab = jnp.transpose(slab, (0, 3, 4, 2, 1)).reshape(2, 2 * PART * PART, RANK).astype(F32)
    result = update(grads, weights, table["pick"], slab)
    return jnp.transpose(result.reshape(2, PART, PART, 2, RANK), (0, 4, 3, 1, 2))


def solution(mesh):
    placed = (
        P(None, None, None, "dev", None),
        P(),
        P(),
        P(("grp", "dev"), None, None, None, None, None),
        P(("grp", "dev"), None),
    )
    return jax.shard_map(
        on_device,
        mesh=mesh,
        in_specs=placed,
        out_specs=P(None, None, None, "dev", "grp"),
        check_vma=False,
    )
```
